512 devices in a mesh: inst: 64 (over x, z, y_hi), tp: 8 (over y_lo, core).
Axes of the slice: x: 4, y: 8 (y_hi: 2, y_lo: 4; y = y_hi * 4 + y_lo), z: 8, core: 2. Of those that a mesh axis runs over, the one named last changes fastest.
Arguments:
- queries: bfloat16 [1024, 8192], P(('inst', 'tp')), may hold values from -32 to 32
- new_kv: bfloat16 [1024, 2048], P(('inst', 'tp')), may hold values from -6 to 6
- kv_pool: bfloat16 [64, 256, 16, 8, 256], P('inst', None, None, 'tp'), may hold values from -8 to 8
- context_lens: int32 [1024], P('inst'), may hold values from 1 to 256, 131072 in all
- block_table: int32 [1024, 16], P('inst'), may hold values from 0 to 255, as said below
- send_pages: int32 [64, 64], P('inst'), may hold values from 0 to 255
- send_dest: int32 [4096, 1], P('inst'), may hold values from 0 to 63; in each aligned block of 64 rows (0 to 63, 64 to 127, ...) at most 2 rows name the same one
- recv_pool: bfloat16 [64, 128, 16, 8, 256], P('inst', None, None, 'tp'), may hold values from -6 to 6
- recv_table: int32 [64, 128], P('inst'), may hold values from 0 to 127, each once within a row
Outputs:
- attended: bfloat16 [1024, 8192], P(('inst', 'tp'))
- landed_pool: bfloat16 [64, 128, 16, 8, 256], P('inst', None, None, 'tp')
The draws below stay inside these ranges and needn't reach their ends.
Inputs may be any that keep to these rules, and one draw needn't show every extreme that they name: `context_lens`: some row has exactly 256 cached tokens. `block_table`: the entries of one instance's rows are pairwise distinct. `send_dest`: among one source's 64 listed pages at most 2 go to any one destination, and in some source's list exactly 2 go to one destination. `recv_table`: each instance's row is a permutation of its receiving slots.
All inputs are finite; a program needn't handle non-finite values. No bound on the sum of `context_lens` on one device may be relied on, other than what follows from the above.
Results may differ from the reference program's by a relative error of at most 0.007.
Values may be sent and summed in bfloat16 or wider, within the bound.
No kernel may reach another device: no remote copies, remote signals or barrier semaphores. Data moves between devices by JAX's collectives and lax.ppermute only.
A program may use at most 64 MiB of HBM per device.

```python
import math
import jax
import jax.numpy as jnp
import numpy as np
from jax import lax

HEADS = 64
KV_HEADS = 8
HEAD_DIM = 128
GROUP = 8
PAGE = 16
MAXP = 16
MOST = 2
ROWS_INST = 16
POOL = 256
ROWS = 1024
MIG = 64
RECV = 128
N_INST = 64


def draw_queries(key, part):
    key = jax.random.fold_in(key, 11)
    first = jax.random.fold_in(key, 0)
    values = jnp.clip(jax.random.normal(first, (ROWS, HEADS * HEAD_DIM), jnp.float32), -6.0, 6.0)
    return values.astype(jnp.bfloat16)


def draw_kv_pool(key, part):
    key = jax.random.fold_in(key, 23)
    shape_all = (N_INST, POOL, PAGE, KV_HEADS, 2 * HEAD_DIM)
    values = jnp.clip(jax.random.normal(key, shape_all, jnp.float32), -6.0, 6.0)
    return values.astype(jnp.bfloat16)


def draw_block_table(key, part):
    key = jax.random.fold_in(key, 37)
    inst_keys = jax.random.split(key, N_INST)
    orders = jax.vmap(lambda single: jax.random.permutation(single, POOL))(inst_keys)
    return orders.reshape(N_INST * ROWS_INST, MAXP).astype(jnp.int32)


def touch_ends(result, stream_key, low, largest):
    longest = result.shape.index(max(result.shape))
    spots = []
    for shift in (0, 1):
        where = [jax.random.randint(jax.random.fold_in(stream_key, axis), (), 0, length) for axis, length in enumerate(result.shape)]
        where[longest] = (where[longest] + shift) % result.shape[longest]
        spots.append(tuple(where))
    return result.at[spots[0]].set(low).at[spots[1]].set(largest)


def shard_levels(key, shape, pieces, smallest, top_value):
    factor_of, own = 1.0, jax.random.fold_in(key, 6)
    for axis_at, parts in pieces:
        steps = jnp.exp(jax.random.uniform(jax.random.fold_in(own, axis_at), (parts,), jnp.float32, smallest / len(pieces), top_value / len(pieces)))
        factor_of = factor_of * jnp.repeat(steps, shape[axis_at] // parts).reshape([-1 if axis == axis_at else 1 for axis in range(len(shape))])
    return factor_of


def split_up(count, total, reach, skew):
    loads = [(1 << 20) // math.isqrt(standing ** skew) + 1 for standing in range(2, count + 1)]
    spare, holding = total - reach - (count - 1), [1] * (count - 1)
    while spare > 0:
        candidates = [i for i in range(count - 1) if holding[i] < reach]
        pool, remaining = sum([loads[i] for i in candidates]), spare
        for i in candidates:
            addition = min(reach - holding[i], max(1, remaining * loads[i] // pool), spare)
            holding[i] = holding[i] + addition
            spare = spare - addition
    return np.array([reach] + holding)


def ragged_sizes(stream_key, number_of, total, limit, slope):
    if number_of == 2:
        one = jax.random.randint(stream_key, (), max(1, total - limit), min(limit, total - 1) + 1)
        return jnp.stack([one, total - one])
    tallies = jnp.asarray(split_up(number_of, total, limit, slope), jnp.int32)
    couples = (number_of - 1) // 2
    source_of, receiver = tallies[1:1 + 2 * couples:2], tallies[2:2 + 2 * couples:2]
    room = jnp.minimum(source_of - 1, limit - receiver)
    moved = jax.random.randint(jax.random.fold_in(stream_key, 1), (couples,), 0, 1 << 20) % (room + 1)
    tallies = tallies.at[1:1 + 2 * couples:2].set(source_of - moved).at[2:2 + 2 * couples:2].set(receiver + moved)
    return tallies[jax.random.permutation(jax.random.fold_in(stream_key, 2), number_of)]


def routed_block(rng, own, number, rows, amount, top, limit, lean):
    ranking = jax.random.permutation(rng, amount)
    crowded, ordinary = shares(amount, rows * top, limit, lean, True), shares(amount, rows * top, limit, lean, False)
    places = jnp.arange(amount)

    def named(sizes, turn):
        used = int((sizes > 0).sum())
        fixed = max(1, used // 4)
        shifted = fixed + (places - fixed + turn * (used - fixed)) % max(1, amount - fixed)
        return jnp.zeros((amount,), jnp.int32).at[ranking[jnp.where(places < fixed, places, shifted)]].set(jnp.asarray(sizes, jnp.int32))

    sizes = jnp.where(number % 4 == 0, named(crowded, number // 4), named(ordinary, number - number // 4 - 1))
    mixed = jax.random.permutation(jax.random.fold_in(own, 3), amount)
    source_of, receiver = mixed[0:amount // 2 * 2:2], mixed[1:amount // 2 * 2:2]
    margin = jnp.minimum(sizes[source_of] - 1, limit - sizes[receiver]) // 2
    margin = jnp.where((source_of == ranking[0]) | (receiver == ranking[0]) | (sizes[receiver] == 0), 0, jnp.maximum(margin, 0))
    shifted = jax.random.randint(jax.random.fold_in(own, 4), (amount // 2,), 0, 1 << 20) % (margin + 1)
    sizes = sizes.at[source_of].add(-shifted).at[receiver].add(shifted)
    labels = jnp.searchsorted(jnp.cumsum(sizes), jnp.arange(rows * top), side="right").astype(jnp.int32)
    grid = labels.reshape(top, rows).T
    grid = grid[jax.random.permutation(jax.random.fold_in(own, 1), rows)]
    turn = jax.random.randint(jax.random.fold_in(own, 2), (rows, 1), 0, top)
    return jnp.take_along_axis(grid, (jnp.arange(top)[None, :] + turn) % top, axis=1)


def shares(number_of, total, limit, slope, full):
    portions = [(1 << 20) // math.isqrt(standing ** slope) + 1 for standing in range(1, number_of + 1)]
    largest = limit if full else min(limit, max(-(-total // number_of), total * portions[0] // sum(portions)))
    least = 1 if total - largest >= number_of - 1 else 0
    holding, spare = [largest] + [least] * (number_of - 1), total - largest - least * (number_of - 1)
    while spare > 0:
        free = [i for i in range(1, number_of) if holding[i] < largest] or [i for i in range(1, number_of) if holding[i] < limit]
        pool, remaining = sum([portions[i] for i in free]), spare
        for i in free:
            more = min(limit - holding[i], max(1, remaining * portions[i] // pool), spare)
            holding[i] = holding[i] + more
            spare = spare - more
    return np.array(holding)


def bell_draw(rng, shape, deviation, limit, shards=(), held_as=jnp.bfloat16):
    level = shard_levels(rng, shape, shards, -0.22, 0.18) if shards else 1.0
    entries = jax.random.normal(rng, shape, jnp.float32) * deviation * level
    return jnp.minimum(jnp.maximum(entries, -limit), limit).astype(held_as)


def setup_inputs(seed: int = 0) -> dict:
    splits = jax.random.split(jax.random.key(seed), 10)
    queries = draw_queries(jax.random.fold_in(splits[9], 71), 0)
    new_kv = bell_draw(splits[1], (ROWS, KV_HEADS * 2 * HEAD_DIM), 1.0, 6.0, ((0, 512),))
    kv_pool = draw_kv_pool(jax.random.fold_in(splits[9], 71), 0)
    context_lens = ragged_sizes(splits[3], ROWS, ROWS * MAXP * PAGE // 2, MAXP * PAGE, 2).astype(jnp.int32)
    block_table = draw_block_table(jax.random.fold_in(splits[9], 71), 0)
    send_pages = touch_ends(jax.random.randint(splits[5], (N_INST, MIG), 0, POOL), jax.random.fold_in(splits[5], 1), 0, POOL - 1).astype(jnp.int32)
    send_dest_keys = jax.random.split(jax.random.fold_in(splits[6], 1), (N_INST * MIG) // MIG)
    send_dest_turns = jax.random.permutation(jax.random.fold_in(splits[6], 3), (N_INST * MIG) // MIG)
    send_dest = jax.vmap(lambda own, number: routed_block(jax.random.fold_in(splits[6], 2), own, number, MIG, N_INST, 1, MOST, 2))(send_dest_keys, send_dest_turns).reshape((N_INST * MIG, 1))
    recv_pool = bell_draw(splits[7], (N_INST, RECV, PAGE, KV_HEADS, 2 * HEAD_DIM), 1.0, 6.0, ((0, 64), (3, 8)))
    recv_table = jax.vmap(lambda own: jax.random.permutation(own, RECV))(jax.random.split(splits[8], N_INST)).reshape((N_INST, RECV)).astype(jnp.int32)
    return {"queries": queries, "new_kv": new_kv, "kv_pool": kv_pool, "context_lens": context_lens, "block_table": block_table, "send_pages": send_pages, "send_dest": send_dest, "recv_pool": recv_pool, "recv_table": recv_table}


def attend_rows(queries, new_kv, kv_pool, context_lens, block_table):
    owners = (jnp.arange(ROWS) // ROWS_INST).astype(jnp.int32)
    score_scale = HEAD_DIM ** -0.5
    tokens_all = MAXP * PAGE

    def one_row(inputs):
        query_row, fresh_row, length, table_row, owner = inputs
        gathered = kv_pool[owner, table_row]
        cache = gathered.reshape(tokens_all, KV_HEADS, 2 * HEAD_DIM).astype(jnp.float32)
        query_f = query_row.astype(jnp.float32).reshape(KV_HEADS, GROUP, HEAD_DIM)
        fresh_f = fresh_row.astype(jnp.float32).reshape(KV_HEADS, 2 * HEAD_DIM)
        scores = jnp.einsum("gjd,tgd->gjt", query_f, cache[:, :, :HEAD_DIM]) * score_scale
        own_score = jnp.einsum("gjd,gd->gj", query_f, fresh_f[:, :HEAD_DIM]) * score_scale
        live = jnp.arange(tokens_all) < length
        row_max = jnp.maximum(jnp.max(jnp.where(live, scores, -1e30), axis=-1), own_score)
        weights_raw = jnp.where(live, jnp.exp(scores - row_max[..., None]), 0.0)
        own_raw = jnp.exp(own_score - row_max)
        weight_sum = jnp.sum(weights_raw, axis=-1) + own_raw
        weights = (weights_raw / weight_sum[..., None]).astype(jnp.bfloat16)
        own_weight = (own_raw / weight_sum).astype(jnp.bfloat16)
        mixed_out = jnp.einsum("gjt,tgd->gjd", weights.astype(jnp.float32), cache[:, :, HEAD_DIM:])
        mixed_out = mixed_out + own_weight.astype(jnp.float32)[..., None] * fresh_f[:, None, HEAD_DIM:]
        return mixed_out.reshape(HEADS * HEAD_DIM).astype(jnp.bfloat16)

    return lax.map(one_row, (queries, new_kv, context_lens, block_table, owners))


def migrate(kv_pool, send_pages, send_dest, recv_pool, recv_table):
    target_inst = send_dest[:, 0].reshape(N_INST, MIG)
    listed = jnp.arange(MIG)
    earlier_same = (target_inst[:, :, None] == target_inst[:, None, :]) & (listed[None, None, :] < listed[None, :, None])
    position = jnp.sum(earlier_same.astype(jnp.int32), axis=-1)
    sources = jnp.arange(N_INST).astype(jnp.int32)[:, None]
    moved = kv_pool[sources, send_pages]
    slot_index = recv_table[target_inst, sources * MOST + position]
    return recv_pool.at[target_inst, slot_index].set(moved)


def reference(queries, new_kv, kv_pool, context_lens, block_table, send_pages, send_dest, recv_pool, recv_table):
    attended = attend_rows(queries, new_kv, kv_pool, context_lens, block_table)
    landed_pool = migrate(kv_pool, send_pages, send_dest, recv_pool, recv_table)
    return attended, landed_pool
```

```python
import functools

import jax
import jax.numpy as jnp
from jax import lax
from jax.experimental import pallas as pl
from jax.experimental.pallas import tpu as pltpu
from jax.sharding import PartitionSpec as P

EMPTY = 256.0
EDGE = 64.0
MASKED = -1e30


def pack_kernel(capacity, pages_ref, dest_ref, pool_ref, out_ref, pages, dest, taken, packed, sems):
    listed = dest.shape[1]
    peers = taken.shape[0]
    lists = (
        pltpu.make_async_copy(pages_ref, pages, sems.at[0]),
        pltpu.make_async_copy(dest_ref, dest, sems.at[1]),
    )
    for copy in lists:
        copy.start()
    packed[...] = jnp.full(packed.shape, EMPTY, packed.dtype)

    def clear(peer, carry):
        taken[peer] = 0
        return carry

    lax.fori_loop(0, peers, clear, 0, unroll=8)
    for copy in lists:
        copy.wait()

    def send(index, carry):
        peer = dest[0, index]
        position = taken[peer]
        taken[peer] = position + 1
        pltpu.make_async_copy(
            pool_ref.at[pages[0, index]], packed.at[peer * capacity + position], sems.at[2]
        ).start()
        return carry

    lax.fori_loop(0, listed, send, 0, unroll=8)
    pltpu.make_async_copy(
        pool_ref.at[pl.ds(0, listed)], packed.at[pl.ds(0, listed)], sems.at[2]
    ).wait()
    done = pltpu.make_async_copy(packed, out_ref, sems.at[0])
    done.start()
    done.wait()


def pack_pages(pool, pages, dest, peers, capacity):
    page_shape = pool.shape[1:]
    listed = dest.shape[1]
    packed_shape = (peers * capacity,) + page_shape
    return pl.pallas_call(
        functools.partial(pack_kernel, capacity),
        out_shape=jax.ShapeDtypeStruct(packed_shape, pool.dtype),
        in_specs=[
            pl.BlockSpec(memory_space=pl.ANY),
            pl.BlockSpec(memory_space=pl.ANY),
            pl.BlockSpec(memory_space=pltpu.HBM),
        ],
        out_specs=pl.BlockSpec(memory_space=pl.ANY),
        scratch_shapes=[
            pltpu.SMEM((1, listed), jnp.int32),
            pltpu.SMEM((1, listed), jnp.int32),
            pltpu.SMEM((peers,), jnp.int32),
            pltpu.VMEM(packed_shape, pool.dtype),
            pltpu.SemaphoreType.DMA((3,)),
        ],
        name="pack_pages",
    )(pages, dest, pool)


def stage_kernel(from_ref, to_ref, sem):
    copy = pltpu.make_async_copy(from_ref, to_ref, sem)
    copy.start()
    copy.wait()


def stage(x):
    return pl.pallas_call(
        stage_kernel,
        out_shape=pltpu.VMEM(x.shape, x.dtype),
        in_specs=[pl.BlockSpec(memory_space=pltpu.HBM)],
        out_specs=pl.BlockSpec(memory_space=pltpu.VMEM),
        scratch_shapes=[pltpu.SemaphoreType.DMA],
        compiler_params=pltpu.CompilerParams(vmem_limit_bytes=16 * 1024 * 1024),
        name="stage_old_pages",
    )(x)


def land_kernel(source_ref, arrived_ref, old_ref, out_ref, landed, sems):
    slots = landed.shape[0]
    parts = sems.shape[0]
    step = slots // parts
    copies = []
    for part in range(parts):

        def place(slot, carry):
            page = arrived_ref[source_ref[slot]]
            landed[slot] = jnp.where(page > EDGE, old_ref[slot], page)
            return carry

        lax.fori_loop(part * step, (part + 1) * step, place, 0, unroll=True)
        copies.append(
            pltpu.make_async_copy(
                landed.at[pl.ds(part * step, step)],
                out_ref.at[pl.ds(part * step, step)],
                sems.at[part],
            )
        )
        copies[-1].start()
    for copy in copies:
        copy.wait()


def land_pages(arrived, old, source):
    return pl.pallas_call(
        land_kernel,
        out_shape=jax.ShapeDtypeStruct(old.shape, old.dtype),
        in_specs=[
            pl.BlockSpec(memory_space=pltpu.SMEM),
            pl.BlockSpec(memory_space=pltpu.VMEM),
            pl.BlockSpec(memory_space=pltpu.VMEM),
        ],
        out_specs=pl.BlockSpec(memory_space=pl.ANY),
        scratch_shapes=[
            pltpu.VMEM(old.shape, old.dtype),
            pltpu.SemaphoreType.DMA((8,)),
        ],
        compiler_params=pltpu.CompilerParams(vmem_limit_bytes=16 * 1024 * 1024),
        name="land_pages",
    )(source, arrived, old)


def attend_kernel(scale, query_ref, fresh_ref, owner_ref, pool_ref, out_ref, score_ref):
    rows = query_ref.shape[0]
    dim = fresh_ref.shape[1] // 2
    group = query_ref.shape[1] // dim
    lanes = owner_ref.shape[1]
    chunk = 4 * lanes
    tokens = pool_ref.shape[0]
    query = jnp.concatenate([query_ref[:, j * dim : (j + 1) * dim] for j in range(group)], axis=0)
    fresh_key = jnp.concatenate([fresh_ref[:, :dim].astype(jnp.float32)] * group, axis=0)
    fresh_value = jnp.concatenate([fresh_ref[:, dim:].astype(jnp.float32)] * group, axis=0)
    own = jnp.sum(query.astype(jnp.float32) * fresh_key, axis=1, keepdims=True) * scale
    row_of = lax.broadcasted_iota(jnp.int32, (group * rows, lanes), 0) % rows
    top = jnp.full((group * rows, lanes), MASKED, jnp.float32)
    for start in range(0, tokens, chunk):
        keys = pool_ref[start : start + chunk, :dim]
        scores = (
            lax.dot_general(
                query, keys, (((1,), (1,)), ((), ())), preferred_element_type=jnp.float32
            )
            * scale
        )
        for part in range(chunk // lanes):
            block = start // lanes + part
            kept = jnp.where(
                owner_ref[block : block + 1, :] == row_of,
                scores[:, part * lanes : (part + 1) * lanes],
                MASKED,
            )
            score_ref[:, block * lanes : (block + 1) * lanes] = kept
            top = jnp.maximum(top, kept)
    top = jnp.maximum(jnp.max(top, axis=1, keepdims=True), own)
    own = jnp.exp(own - top)
    total = jnp.zeros((group * rows, lanes), jnp.float32)
    mixed = jnp.zeros((group * rows, dim), jnp.float32)
    for start in range(0, tokens, chunk):
        weights = jnp.exp(score_ref[:, start : start + chunk] - top)
        for part in range(chunk // lanes):
            total = total + weights[:, part * lanes : (part + 1) * lanes]
        mixed = mixed + jnp.dot(
            weights.astype(jnp.bfloat16),
            pool_ref[start : start + chunk, dim:],
            preferred_element_type=jnp.float32,
        )
    total = jnp.sum(total, axis=1, keepdims=True) + own
    mixed = (mixed + own.astype(jnp.bfloat16).astype(jnp.float32) * fresh_value) / total
    mixed = mixed.astype(out_ref.dtype)
    for j in range(group):
        out_ref[:, j * dim : (j + 1) * dim] = mixed[j * rows : (j + 1) * rows]


def attend(query, fresh, owner, pool, scale):
    rows, dim = query.shape[0], fresh.shape[1] // 2
    group = query.shape[1] // dim
    tokens = pool.shape[0]
    return pl.pallas_call(
        functools.partial(attend_kernel, scale),
        out_shape=jax.ShapeDtypeStruct(query.shape, query.dtype),
        in_specs=[pl.BlockSpec(memory_space=pltpu.VMEM)] * 4,
        out_specs=pl.BlockSpec(memory_space=pltpu.VMEM),
        scratch_shapes=[pltpu.VMEM((rows * group, tokens), jnp.float32)],
        compiler_params=pltpu.CompilerParams(vmem_limit_bytes=24 * 1024 * 1024),
        cost_estimate=pl.CostEstimate(
            flops=4 * rows * group * tokens * dim,
            bytes_accessed=pool.size * 2,
            transcendentals=rows * group * tokens,
        ),
        name="attend",
    )(query, fresh, owner, pool)


def token_owners(lengths, table, pages, page_size):
    rows, per_row = table.shape
    block = jnp.arange(rows * per_row, dtype=jnp.int32)
    row = block // per_row
    live = jnp.clip(
        (lengths[:, None] - jnp.arange(per_row, dtype=jnp.int32)[None, :] * page_size),
        0,
        page_size,
    ).reshape(-1)
    coded = row * (2 * page_size) + live
    page = jnp.arange(pages, dtype=jnp.int32)
    of_page = jnp.sum(
        jnp.where(table.reshape(-1)[None, :] == page[:, None], coded[None, :], 0), axis=1
    )
    per_line = 128 // page_size
    offset = jnp.arange(page_size, dtype=jnp.int32)
    of_page = of_page.reshape(pages // per_line, per_line, 1)
    owner = jnp.where(offset < of_page % (2 * page_size), of_page // (2 * page_size), -1)
    return owner.reshape(pages // per_line, 128)


def pair_gather(x):
    groups = lax.axis_size("tp")
    chips = [[2 * i, 2 * i + 1] for i in range(groups // 2)]
    return lax.all_gather(x, "tp", axis=0, tiled=False, axis_index_groups=chips)


def chip_exchange(pieces):
    groups = lax.axis_size("tp")
    chip = lax.axis_index("tp") // 2
    chips = pieces.shape[0]
    got = [lax.dynamic_index_in_dim(pieces, chip, 0, keepdims=False)]
    for k in range(1, chips):
        piece = lax.dynamic_index_in_dim(pieces, chip ^ k, 0, keepdims=False)
        got.append(lax.ppermute(piece, "tp", [(i, i ^ (2 * k)) for i in range(groups)]))
    stacked = jnp.stack(got)
    order = chip ^ jnp.arange(chips)
    return jnp.stack([lax.dynamic_index_in_dim(stacked, chip ^ k, 0, keepdims=False) for k in range(chips)])


def gather_queries(queries, new_kv):
    groups = lax.axis_size("tp")
    rows_local = queries.shape[0]
    split = jnp.concatenate([queries.reshape(rows_local, groups, -1), new_kv.reshape(rows_local, groups, -1)], axis=2)
    got = lax.all_to_all(split, "tp", split_axis=1, concat_axis=0, tiled=True)
    return got.reshape(groups * rows_local, -1)


def return_heads(mixed, me):
    groups = lax.axis_size("tp")
    rows, width = mixed.shape
    rows_local = rows // groups
    both = pair_gather(mixed)
    both = both.reshape(2, groups // 2, 2, rows_local, width)
    mine = lax.dynamic_index_in_dim(both, me % 2, 2, keepdims=False)
    got = chip_exchange(mine.transpose(1, 0, 2, 3))
    return got.reshape(groups, rows_local, width).transpose(1, 0, 2).reshape(rows_local, -1)


def on_device(
    queries,
    new_kv,
    kv_pool,
    context_lens,
    block_table,
    send_pages,
    send_dest,
    recv_pool,
    recv_table,
):
    groups = lax.axis_size("tp")
    peers = lax.axis_size("inst")
    me = lax.axis_index("tp")
    _, pages, page_size, kv_local, width = kv_pool.shape
    dim = width // 2
    heads_width = queries.shape[1] // groups
    slots = recv_table.shape[1]
    pool = kv_pool.reshape(pages, page_size, width)

    both = gather_queries(queries, new_kv)
    outgoing = pack_pages(pool, send_pages, send_dest.reshape(1, -1), peers, slots // peers)
    both, outgoing = lax.optimization_barrier((both, outgoing))
    arrived = lax.all_to_all(outgoing, "inst", split_axis=0, concat_axis=0, tiled=True)

    owner = token_owners(context_lens, block_table, pages, page_size)
    mixed = attend(
        both[:, :heads_width],
        both[:, heads_width:],
        owner,
        pool.reshape(pages * page_size, width),
        dim ** (-0.5),
    )
    attended = return_heads(mixed, me)

    slot = jnp.arange(slots, dtype=jnp.int32)
    source = jnp.sum(
        jnp.where(recv_table[0][None, :] == slot[:, None], slot[None, :], 0), axis=1
    )
    mixed, recv_pool = lax.optimization_barrier((mixed, recv_pool))
    old = stage(recv_pool.reshape(slots, page_size, width))
    landed = land_pages(arrived, old, source)
    return (attended, landed.reshape(recv_pool.shape))


def solution(mesh):
    return jax.shard_map(
        on_device,
        mesh=mesh,
        in_specs=(
            P(("inst", "tp"), None),
            P(("inst", "tp"), None),
            P("inst", None, None, "tp", None),
            P("inst"),
            P("inst", None),
            P("inst", None),
            P("inst", None),
            P("inst", None, None, "tp", None),
            P("inst", None),
        ),
        out_specs=(P(("inst", "tp"), None), P("inst", None, None, "tp", None)),
        check_vma=False,
    )
```

```python
import functools

import jax
import jax.numpy as jnp
from jax import lax
from jax.experimental import pallas as pl
from jax.experimental.pallas import tpu as pltpu
from jax.sharding import PartitionSpec as P

EMPTY = 256.0
EDGE = 64.0
MASKED = -1e30
LEVEL_PARTS = 3


def pack_kernel(capacity, pages_ref, dest_ref, pool_ref, out_ref, pages, dest, taken, packed, sems):
    listed = dest.shape[1]
    peers = taken.shape[0]
    lists = (
        pltpu.make_async_copy(pages_ref, pages, sems.at[0]),
        pltpu.make_async_copy(dest_ref, dest, sems.at[1]),
    )
    for copy in lists:
        copy.start()
    packed[...] = jnp.full(packed.shape, EMPTY, packed.dtype)

    def clear(peer, carry):
        taken[peer] = 0
        return carry

    lax.fori_loop(0, peers, clear, 0, unroll=8)
    for copy in lists:
        copy.wait()

    def send(index, carry):
        peer = dest[0, index]
        position = taken[peer]
        taken[peer] = position + 1
        pltpu.make_async_copy(
            pool_ref.at[pages[0, index]], packed.at[peer * capacity + position], sems.at[2]
        ).start()
        return carry

    lax.fori_loop(0, listed, send, 0, unroll=8)
    pltpu.make_async_copy(
        pool_ref.at[pl.ds(0, listed)], packed.at[pl.ds(0, listed)], sems.at[2]
    ).wait()
    done = pltpu.make_async_copy(packed, out_ref, sems.at[0])
    done.start()
    done.wait()


def pack_pages(pool, pages, dest, peers, capacity):
    page_shape = pool.shape[1:]
    listed = dest.shape[1]
    packed_shape = (peers * capacity,) + page_shape
    return pl.pallas_call(
        functools.partial(pack_kernel, capacity),
        out_shape=jax.ShapeDtypeStruct(packed_shape, pool.dtype),
        in_specs=[
            pl.BlockSpec(memory_space=pl.ANY),
            pl.BlockSpec(memory_space=pl.ANY),
            pl.BlockSpec(memory_space=pltpu.HBM),
        ],
        out_specs=pl.BlockSpec(memory_space=pl.ANY),
        scratch_shapes=[
            pltpu.SMEM((1, listed), jnp.int32),
            pltpu.SMEM((1, listed), jnp.int32),
            pltpu.SMEM((peers,), jnp.int32),
            pltpu.VMEM(packed_shape, pool.dtype),
            pltpu.SemaphoreType.DMA((3,)),
        ],
        name="pack_pages",
    )(pages, dest, pool)


def stage_kernel(from_ref, to_ref, sem):
    copy = pltpu.make_async_copy(from_ref, to_ref, sem)
    copy.start()
    copy.wait()


def stage(x):
    return pl.pallas_call(
        stage_kernel,
        out_shape=pltpu.VMEM(x.shape, x.dtype),
        in_specs=[pl.BlockSpec(memory_space=pltpu.HBM)],
        out_specs=pl.BlockSpec(memory_space=pltpu.VMEM),
        scratch_shapes=[pltpu.SemaphoreType.DMA],
        compiler_params=pltpu.CompilerParams(vmem_limit_bytes=16 * 1024 * 1024),
        name="stage_old_pages",
    )(x)


def land_kernel(source_ref, arrived_ref, old_ref, out_ref, landed, sems):
    slots = landed.shape[0]
    parts = sems.shape[0]
    step = slots // parts
    copies = []
    for part in range(parts):

        def place(slot, carry):
            page = arrived_ref[source_ref[slot]]
            landed[slot] = jnp.where(page > EDGE, old_ref[slot], page)
            return carry

        lax.fori_loop(part * step, (part + 1) * step, place, 0, unroll=True)
        copies.append(
            pltpu.make_async_copy(
                landed.at[pl.ds(part * step, step)],
                out_ref.at[pl.ds(part * step, step)],
                sems.at[part],
            )
        )
        copies[-1].start()
    for copy in copies:
        copy.wait()


def land_pages(arrived, old, source):
    return pl.pallas_call(
        land_kernel,
        out_shape=jax.ShapeDtypeStruct(old.shape, old.dtype),
        in_specs=[
            pl.BlockSpec(memory_space=pltpu.SMEM),
            pl.BlockSpec(memory_space=pltpu.VMEM),
            pl.BlockSpec(memory_space=pltpu.VMEM),
        ],
        out_specs=pl.BlockSpec(memory_space=pl.ANY),
        scratch_shapes=[
            pltpu.VMEM(old.shape, old.dtype),
            pltpu.SemaphoreType.DMA((8,)),
        ],
        compiler_params=pltpu.CompilerParams(vmem_limit_bytes=16 * 1024 * 1024),
        name="land_pages",
    )(source, arrived, old)


def attend_kernel(scale, query_ref, owner_ref, pool_ref, out_ref, score_ref):
    rows = query_ref.shape[0]
    dim = pool_ref.shape[1] // 2
    group = query_ref.shape[1] // dim
    lanes = owner_ref.shape[1]
    chunk = 4 * lanes
    tokens = pool_ref.shape[0]
    query = jnp.concatenate([query_ref[:, j * dim : (j + 1) * dim] for j in range(group)], axis=0)
    row_of = lax.broadcasted_iota(jnp.int32, (group * rows, lanes), 0) % rows
    top = jnp.full((group * rows, lanes), MASKED, jnp.float32)
    for start in range(0, tokens, chunk):
        keys = pool_ref[start : start + chunk, :dim]
        scores = (
            lax.dot_general(
                query, keys, (((1,), (1,)), ((), ())), preferred_element_type=jnp.float32
            )
            * scale
        )
        for part in range(chunk // lanes):
            block = start // lanes + part
            kept = jnp.where(
                owner_ref[block : block + 1, :] == row_of,
                scores[:, part * lanes : (part + 1) * lanes],
                MASKED,
            )
            score_ref[:, block * lanes : (block + 1) * lanes] = kept
            top = jnp.maximum(top, kept)
    top = jnp.max(top, axis=1, keepdims=True)
    total = jnp.zeros((group * rows, lanes), jnp.float32)
    mixed = jnp.zeros((group * rows, dim), jnp.float32)
    for start in range(0, tokens, chunk):
        weights = jnp.exp(score_ref[:, start : start + chunk] - top)
        for part in range(chunk // lanes):
            total = total + weights[:, part * lanes : (part + 1) * lanes]
        mixed = mixed + jnp.dot(
            weights.astype(jnp.bfloat16),
            pool_ref[start : start + chunk, dim:],
            preferred_element_type=jnp.float32,
        )
    total = jnp.sum(total, axis=1, keepdims=True)
    mixed = (mixed / total).astype(out_ref.dtype)
    level = top + jnp.log(total)
    lane = lax.broadcasted_iota(jnp.int32, (rows, lanes), 1)
    levels = jnp.zeros((rows, lanes), jnp.float32)
    for j in range(group):
        out_ref[:, j * dim : (j + 1) * dim] = mixed[j * rows : (j + 1) * rows]
        rest = level[j * rows : (j + 1) * rows]
        for part in range(LEVEL_PARTS):
            piece = rest.astype(out_ref.dtype).astype(jnp.float32)
            levels = jnp.where(lane == part * group + j, piece, levels)
            rest = rest - piece
    out_ref[:, group * dim :] = levels.astype(out_ref.dtype)


def attend(query, owner, pool, scale):
    rows, dim = query.shape[0], pool.shape[1] // 2
    group = query.shape[1] // dim
    tokens = pool.shape[0]
    return pl.pallas_call(
        functools.partial(attend_kernel, scale),
        out_shape=jax.ShapeDtypeStruct((rows, group * dim + 128), query.dtype),
        in_specs=[pl.BlockSpec(memory_space=pltpu.VMEM)] * 3,
        out_specs=pl.BlockSpec(memory_space=pltpu.VMEM),
        scratch_shapes=[pltpu.VMEM((rows * group, tokens), jnp.float32)],
        compiler_params=pltpu.CompilerParams(vmem_limit_bytes=24 * 1024 * 1024),
        cost_estimate=pl.CostEstimate(
            flops=4 * rows * group * tokens * dim,
            bytes_accessed=pool.size * 2,
            transcendentals=rows * group * tokens,
        ),
        name="attend",
    )(query, owner, pool)


def token_owners(lengths, table, pages, page_size):
    rows, per_row = table.shape
    block = jnp.arange(rows * per_row, dtype=jnp.int32)
    row = block // per_row
    live = jnp.clip(
        (lengths[:, None] - jnp.arange(per_row, dtype=jnp.int32)[None, :] * page_size),
        0,
        page_size,
    ).reshape(-1)
    coded = row * (2 * page_size) + live
    page = jnp.arange(pages, dtype=jnp.int32)
    of_page = jnp.sum(
        jnp.where(table.reshape(-1)[None, :] == page[:, None], coded[None, :], 0), axis=1
    )
    per_line = 128 // page_size
    offset = jnp.arange(page_size, dtype=jnp.int32)
    of_page = of_page.reshape(pages // per_line, per_line, 1)
    owner = jnp.where(offset < of_page % (2 * page_size), of_page // (2 * page_size), -1)
    return owner.reshape(pages // per_line, 128)


def pair_gather(x):
    groups = lax.axis_size("tp")
    chips = [[2 * i, 2 * i + 1] for i in range(groups // 2)]
    return lax.all_gather(x, "tp", axis=0, tiled=False, axis_index_groups=chips)


def chip_exchange(pieces):
    groups = lax.axis_size("tp")
    chip = lax.axis_index("tp") // 2
    chips = pieces.shape[0]
    got = [lax.dynamic_index_in_dim(pieces, chip, 0, keepdims=False)]
    for k in range(1, chips):
        piece = lax.dynamic_index_in_dim(pieces, chip ^ k, 0, keepdims=False)
        got.append(lax.ppermute(piece, "tp", [(i, i ^ (2 * k)) for i in range(groups)]))
    return got


def gather_queries(queries):
    groups = lax.axis_size("tp")
    rows = queries.shape[0]
    split = queries.reshape(rows, groups, -1)
    got = lax.all_to_all(split, "tp", split_axis=1, concat_axis=0, tiled=True)
    return got.reshape(groups * rows, -1)


def return_heads(mixed, me):
    groups = lax.axis_size("tp")
    rows, width = mixed.shape
    rows_local = rows // groups
    both = pair_gather(mixed)
    both = both.reshape(2, groups // 2, 2, rows_local, width)
    mine = lax.dynamic_index_in_dim(both, me % 2, 2, keepdims=False)
    return chip_exchange(mine.transpose(1, 0, 2, 3))


def add_new_kernel(dim, scale, chip_ref, query_ref, fresh_ref, *refs):
    pieces, out_ref = refs[:-1], refs[-1]
    heads, _, width = pieces[0].shape
    lanes = 128
    group = (width - lanes) // dim
    chip = chip_ref[0]
    lane = lax.broadcasted_iota(jnp.int32, (pieces[0].shape[1], lanes), 1)
    results = []
    for k, piece in enumerate(pieces):
        for h in range(heads):
            place = (chip ^ k) * heads + h
            fresh = pl.multiple_of(place * (2 * dim), 2 * dim)
            fresh_key = fresh_ref[:, pl.ds(fresh, dim)].astype(jnp.float32)
            fresh_value = fresh_ref[:, pl.ds(fresh + dim, dim)].astype(jnp.float32)
            parts = piece[h, :, group * dim :].astype(jnp.float32)
            level = parts
            for part in range(1, LEVEL_PARTS):
                level = level + pltpu.roll(parts, lanes - part * group, 1)
            own = jnp.zeros_like(level)
            places = []
            for j in range(group):
                places.append(pl.multiple_of(place * (group * dim) + j * dim, dim))
                query = query_ref[:, pl.ds(places[-1], dim)].astype(jnp.float32)
                score = jnp.sum(query * fresh_key, axis=1, keepdims=True) * scale
                own = jnp.where(lane == j, score, own)
            top = jnp.maximum(level, own)
            cached, new = jnp.exp(level - top), jnp.exp(own - top)
            total = cached + new
            cached, new = cached / total, new / total
            for j in range(group):
                value = piece[h, :, j * dim : (j + 1) * dim].astype(jnp.float32)
                mixed = value * cached[:, j : j + 1] + fresh_value * new[:, j : j + 1]
                results.append((places[j], mixed.astype(out_ref.dtype)))
    for at, mixed in results:
        out_ref[:, pl.ds(at, dim)] = mixed


def add_new_token(pieces, queries, new_kv, dim, scale):
    chip = (lax.axis_index("tp") // 2).astype(jnp.int32).reshape(1)
    vmem = pl.BlockSpec(memory_space=pltpu.VMEM)
    return pl.pallas_call(
        functools.partial(add_new_kernel, dim, scale),
        out_shape=jax.ShapeDtypeStruct(queries.shape, queries.dtype),
        in_specs=[pl.BlockSpec(memory_space=pltpu.SMEM)] + [vmem] * (2 + len(pieces)),
        out_specs=vmem,
        compiler_params=pltpu.CompilerParams(vmem_limit_bytes=16 * 1024 * 1024),
        cost_estimate=pl.CostEstimate(
            flops=8 * queries.size,
            bytes_accessed=4 * queries.size,
            transcendentals=2 * queries.size // dim,
        ),
        name="add_new_token",
    )(chip, queries, new_kv, *pieces)


def on_device(
    queries,
    new_kv,
    kv_pool,
    context_lens,
    block_table,
    send_pages,
    send_dest,
    recv_pool,
    recv_table,
):
    peers = lax.axis_size("inst")
    me = lax.axis_index("tp")
    _, pages, page_size, kv_local, width = kv_pool.shape
    dim = width // 2
    slots = recv_table.shape[1]
    pool = kv_pool.reshape(pages, page_size, width)

    query = gather_queries(queries)
    outgoing = pack_pages(pool, send_pages, send_dest.reshape(1, -1), peers, slots // peers)
    query, outgoing = lax.optimization_barrier((query, outgoing))
    arrived = lax.all_to_all(outgoing, "inst", split_axis=0, concat_axis=0, tiled=True)

    owner = token_owners(context_lens, block_table, pages, page_size)
    scale = dim ** (-0.5)
    mixed = attend(query, owner, pool.reshape(pages * page_size, width), scale)
    returned = return_heads(mixed, me)
    attended = add_new_token(returned, queries, new_kv, dim, scale)

    slot = jnp.arange(slots, dtype=jnp.int32)
    source = jnp.sum(
        jnp.where(recv_table[0][None, :] == slot[:, None], slot[None, :], 0), axis=1
    )
    mixed, recv_pool = lax.optimization_barrier((mixed, recv_pool))
    old = stage(recv_pool.reshape(slots, page_size, width))
    landed = land_pages(arrived, old, source)
    return (attended, landed.reshape(recv_pool.shape))


def solution(mesh):
    return jax.shard_map(
        on_device,
        mesh=mesh,
        in_specs=(
            P(("inst", "tp"), None),
            P(("inst", "tp"), None),
            P("inst", None, None, "tp", None),
            P("inst"),
            P("inst", None),
            P("inst", None),
            P("inst", None),
            P("inst", None, None, "tp", None),
            P("inst", None),
        ),
        out_specs=(P(("inst", "tp"), None), P("inst", None, None, "tp", None)),
        check_vma=False,
    )
```

```python
import functools

import jax
import jax.numpy as jnp
from jax import lax
from jax.experimental import pallas as pl
from jax.experimental.pallas import tpu as pltpu
from jax.sharding import PartitionSpec as P

EMPTY = 256.0
EDGE = 64.0
MASKED = -1e30
LEVEL_PARTS = 3


def place_of(inst):
    x, z, half = inst // 16, inst // 2 % 8, inst % 2
    return (1 - half) * 32 + (7 - z) * 4 + x


def pack_kernel(capacity, pages_ref, dest_ref, pool_ref, out_ref, pages, dest, taken, packed, sems):
    listed = dest.shape[1]
    peers = taken.shape[0]
    lists = (
        pltpu.make_async_copy(pages_ref, pages, sems.at[0]),
        pltpu.make_async_copy(dest_ref, dest, sems.at[1]),
    )
    for copy in lists:
        copy.start()
    packed[...] = jnp.full(packed.shape, EMPTY, packed.dtype)

    def clear(peer, carry):
        taken[peer] = 0
        return carry

    lax.fori_loop(0, peers, clear, 0, unroll=8)
    for copy in lists:
        copy.wait()

    def send(index, carry):
        peer = dest[0, index]
        position = taken[peer]
        taken[peer] = position + 1
        pltpu.make_async_copy(
            pool_ref.at[pages[0, index]],
            packed.at[place_of(peer) * capacity + position],
            sems.at[2],
        ).start()
        return carry

    lax.fori_loop(0, listed, send, 0, unroll=8)
    pltpu.make_async_copy(
        pool_ref.at[pl.ds(0, listed)], packed.at[pl.ds(0, listed)], sems.at[2]
    ).wait()
    done = pltpu.make_async_copy(packed, out_ref, sems.at[0])
    done.start()
    done.wait()


def pack_pages(pool, pages, dest, peers, capacity):
    page_shape = pool.shape[1:]
    listed = dest.shape[1]
    packed_shape = (peers * capacity,) + page_shape
    return pl.pallas_call(
        functools.partial(pack_kernel, capacity),
        out_shape=jax.ShapeDtypeStruct(packed_shape, pool.dtype),
        in_specs=[
            pl.BlockSpec(memory_space=pl.ANY),
            pl.BlockSpec(memory_space=pl.ANY),
            pl.BlockSpec(memory_space=pltpu.HBM),
        ],
        out_specs=pl.BlockSpec(memory_space=pl.ANY),
        scratch_shapes=[
            pltpu.SMEM((1, listed), jnp.int32),
            pltpu.SMEM((1, listed), jnp.int32),
            pltpu.SMEM((peers,), jnp.int32),
            pltpu.VMEM(packed_shape, pool.dtype),
            pltpu.SemaphoreType.DMA((3,)),
        ],
        name="pack_pages",
    )(pages, dest, pool)


def stage_kernel(from_ref, to_ref, sem):
    copy = pltpu.make_async_copy(from_ref, to_ref, sem)
    copy.start()
    copy.wait()


def stage(x):
    return pl.pallas_call(
        stage_kernel,
        out_shape=pltpu.VMEM(x.shape, x.dtype),
        in_specs=[pl.BlockSpec(memory_space=pltpu.HBM)],
        out_specs=pl.BlockSpec(memory_space=pltpu.VMEM),
        scratch_shapes=[pltpu.SemaphoreType.DMA],
        compiler_params=pltpu.CompilerParams(vmem_limit_bytes=16 * 1024 * 1024),
        name="stage_old_pages",
    )(x)


def land_kernel(source_ref, arrived_ref, old_ref, out_ref, landed, sems):
    slots = landed.shape[0]
    parts = sems.shape[0]
    step = slots // parts
    copies = []
    for part in range(parts):

        def place(slot, carry):
            page = arrived_ref[source_ref[slot]]
            landed[slot] = jnp.where(page > EDGE, old_ref[slot], page)
            return carry

        lax.fori_loop(part * step, (part + 1) * step, place, 0, unroll=True)
        copies.append(
            pltpu.make_async_copy(
                landed.at[pl.ds(part * step, step)],
                out_ref.at[pl.ds(part * step, step)],
                sems.at[part],
            )
        )
        copies[-1].start()
    for copy in copies:
        copy.wait()


def land_pages(arrived, old, source):
    return pl.pallas_call(
        land_kernel,
        out_shape=jax.ShapeDtypeStruct(old.shape, old.dtype),
        in_specs=[
            pl.BlockSpec(memory_space=pltpu.SMEM),
            pl.BlockSpec(memory_space=pltpu.VMEM),
            pl.BlockSpec(memory_space=pltpu.VMEM),
        ],
        out_specs=pl.BlockSpec(memory_space=pl.ANY),
        scratch_shapes=[
            pltpu.VMEM(old.shape, old.dtype),
            pltpu.SemaphoreType.DMA((8,)),
        ],
        compiler_params=pltpu.CompilerParams(vmem_limit_bytes=16 * 1024 * 1024),
        name="land_pages",
    )(source, arrived, old)


def attend_kernel(scale, query_ref, owner_ref, pool_ref, out_ref, score_ref):
    rows = query_ref.shape[0]
    dim = pool_ref.shape[1] // 2
    group = query_ref.shape[1] // dim
    lanes = owner_ref.shape[1]
    chunk = 4 * lanes
    tokens = pool_ref.shape[0]
    query = jnp.concatenate([query_ref[:, j * dim : (j + 1) * dim] for j in range(group)], axis=0)
    row_of = lax.broadcasted_iota(jnp.int32, (group * rows, lanes), 0) % rows
    top = jnp.full((group * rows, lanes), MASKED, jnp.float32)
    for start in range(0, tokens, chunk):
        keys = pool_ref[start : start + chunk, :dim]
        scores = (
            lax.dot_general(
                query, keys, (((1,), (1,)), ((), ())), preferred_element_type=jnp.float32
            )
            * scale
        )
        for part in range(chunk // lanes):
            block = start // lanes + part
            kept = jnp.where(
                owner_ref[block : block + 1, :] == row_of,
                scores[:, part * lanes : (part + 1) * lanes],
                MASKED,
            )
            score_ref[:, block * lanes : (block + 1) * lanes] = kept
            top = jnp.maximum(top, kept)
    top = jnp.max(top, axis=1, keepdims=True)
    total = jnp.zeros((group * rows, lanes), jnp.float32)
    mixed = jnp.zeros((group * rows, dim), jnp.float32)
    for start in range(0, tokens, chunk):
        weights = jnp.exp(score_ref[:, start : start + chunk] - top)
        for part in range(chunk // lanes):
            total = total + weights[:, part * lanes : (part + 1) * lanes]
        mixed = mixed + jnp.dot(
            weights.astype(jnp.bfloat16),
            pool_ref[start : start + chunk, dim:],
            preferred_element_type=jnp.float32,
        )
    total = jnp.sum(total, axis=1, keepdims=True)
    mixed = (mixed / total).astype(out_ref.dtype)
    level = top + jnp.log(total)
    lane = lax.broadcasted_iota(jnp.int32, (rows, lanes), 1)
    levels = jnp.zeros((rows, lanes), jnp.float32)
    for j in range(group):
        out_ref[:, j * dim : (j + 1) * dim] = mixed[j * rows : (j + 1) * rows]
        rest = level[j * rows : (j + 1) * rows]
        for part in range(LEVEL_PARTS):
            piece = rest.astype(out_ref.dtype).astype(jnp.float32)
            levels = jnp.where(lane == part * group + j, piece, levels)
            rest = rest - piece
    out_ref[:, group * dim :] = levels.astype(out_ref.dtype)


def attend(query, owner, pool, scale):
    rows, dim = query.shape[0], pool.shape[1] // 2
    group = query.shape[1] // dim
    tokens = pool.shape[0]
    return pl.pallas_call(
        functools.partial(attend_kernel, scale),
        out_shape=jax.ShapeDtypeStruct((rows, group * dim + 128), query.dtype),
        in_specs=[pl.BlockSpec(memory_space=pltpu.VMEM)] * 3,
        out_specs=pl.BlockSpec(memory_space=pltpu.VMEM),
        scratch_shapes=[pltpu.VMEM((rows * group, tokens), jnp.float32)],
        compiler_params=pltpu.CompilerParams(vmem_limit_bytes=24 * 1024 * 1024),
        cost_estimate=pl.CostEstimate(
            flops=4 * rows * group * tokens * dim,
            bytes_accessed=pool.size * 2,
            transcendentals=rows * group * tokens,
        ),
        name="attend",
    )(query, owner, pool)


def token_owners(lengths, table, pages, page_size):
    rows, per_row = table.shape
    block = jnp.arange(rows * per_row, dtype=jnp.int32)
    row = block // per_row
    live = jnp.clip(
        (lengths[:, None] - jnp.arange(per_row, dtype=jnp.int32)[None, :] * page_size),
        0,
        page_size,
    ).reshape(-1)
    coded = row * (2 * page_size) + live
    page = jnp.arange(pages, dtype=jnp.int32)
    of_page = jnp.sum(
        jnp.where(table.reshape(-1)[None, :] == page[:, None], coded[None, :], 0), axis=1
    )
    per_line = 128 // page_size
    offset = jnp.arange(page_size, dtype=jnp.int32)
    of_page = of_page.reshape(pages // per_line, per_line, 1)
    owner = jnp.where(offset < of_page % (2 * page_size), of_page // (2 * page_size), -1)
    return owner.reshape(pages // per_line, 128)


def pair_gather(x):
    groups = lax.axis_size("tp")
    chips = [[2 * i, 2 * i + 1] for i in range(groups // 2)]
    return lax.all_gather(x, "tp", axis=0, tiled=False, axis_index_groups=chips)


def chip_exchange(pieces):
    groups = lax.axis_size("tp")
    chip = lax.axis_index("tp") // 2
    chips = pieces.shape[0]
    got = [lax.dynamic_index_in_dim(pieces, chip, 0, keepdims=False)]
    for k in range(1, chips):
        piece = lax.dynamic_index_in_dim(pieces, chip ^ k, 0, keepdims=False)
        got.append(lax.ppermute(piece, "tp", [(i, i ^ (2 * k)) for i in range(groups)]))
    return got


def gather_queries(queries):
    groups = lax.axis_size("tp")
    rows = queries.shape[0]
    split = queries.reshape(rows, groups, -1)
    got = lax.all_to_all(split, "tp", split_axis=1, concat_axis=0, tiled=True)
    return got.reshape(groups * rows, -1)


def return_heads(mixed, me):
    groups = lax.axis_size("tp")
    rows, width = mixed.shape
    rows_local = rows // groups
    both = pair_gather(mixed)
    both = both.reshape(2, groups // 2, 2, rows_local, width)
    mine = lax.dynamic_index_in_dim(both, me % 2, 2, keepdims=False)
    return chip_exchange(mine.transpose(1, 0, 2, 3))


def add_new_kernel(dim, scale, chip_ref, query_ref, fresh_ref, *refs):
    pieces, out_ref = refs[:-1], refs[-1]
    heads, _, width = pieces[0].shape
    lanes = 128
    group = (width - lanes) // dim
    chip = chip_ref[0]
    lane = lax.broadcasted_iota(jnp.int32, (pieces[0].shape[1], lanes), 1)
    results = []
    for k, piece in enumerate(pieces):
        for h in range(heads):
            place = (chip ^ k) * heads + h
            fresh = pl.multiple_of(place * (2 * dim), 2 * dim)
            fresh_key = fresh_ref[:, pl.ds(fresh, dim)].astype(jnp.float32)
            fresh_value = fresh_ref[:, pl.ds(fresh + dim, dim)].astype(jnp.float32)
            parts = piece[h, :, group * dim :].astype(jnp.float32)
            level = parts
            for part in range(1, LEVEL_PARTS):
                level = level + pltpu.roll(parts, lanes - part * group, 1)
            own = jnp.zeros_like(level)
            places = []
            for j in range(group):
                places.append(pl.multiple_of(place * (group * dim) + j * dim, dim))
                query = query_ref[:, pl.ds(places[-1], dim)].astype(jnp.float32)
                score = jnp.sum(query * fresh_key, axis=1, keepdims=True) * scale
                own = jnp.where(lane == j, score, own)
            top = jnp.maximum(level, own)
            cached, new = jnp.exp(level - top), jnp.exp(own - top)
            total = cached + new
            cached, new = cached / total, new / total
            for j in range(group):
                value = piece[h, :, j * dim : (j + 1) * dim].astype(jnp.float32)
                mixed = value * cached[:, j : j + 1] + fresh_value * new[:, j : j + 1]
                results.append((places[j], mixed.astype(out_ref.dtype)))
    for at, mixed in results:
        out_ref[:, pl.ds(at, dim)] = mixed


def add_new_token(pieces, queries, new_kv, dim, scale):
    chip = (lax.axis_index("tp") // 2).astype(jnp.int32).reshape(1)
    vmem = pl.BlockSpec(memory_space=pltpu.VMEM)
    return pl.pallas_call(
        functools.partial(add_new_kernel, dim, scale),
        out_shape=jax.ShapeDtypeStruct(queries.shape, queries.dtype),
        in_specs=[pl.BlockSpec(memory_space=pltpu.SMEM)] + [vmem] * (2 + len(pieces)),
        out_specs=vmem,
        compiler_params=pltpu.CompilerParams(vmem_limit_bytes=16 * 1024 * 1024),
        cost_estimate=pl.CostEstimate(
            flops=8 * queries.size,
            bytes_accessed=4 * queries.size,
            transcendentals=2 * queries.size // dim,
        ),
        name="add_new_token",
    )(chip, queries, new_kv, *pieces)


def on_device(
    queries,
    new_kv,
    kv_pool,
    context_lens,
    block_table,
    send_pages,
    send_dest,
    recv_pool,
    recv_table,
):
    peers = lax.axis_size("inst")
    me = lax.axis_index("tp")
    _, pages, page_size, kv_local, width = kv_pool.shape
    dim = width // 2
    slots = recv_table.shape[1]
    pool = kv_pool.reshape(pages, page_size, width)

    query = gather_queries(queries)
    outgoing = pack_pages(pool, send_pages, send_dest.reshape(1, -1), peers, slots // peers)
    query, outgoing = lax.optimization_barrier((query, outgoing))
    order = sorted(range(peers), key=place_of)
    arrived = lax.all_to_all(
        outgoing, "inst", split_axis=0, concat_axis=0, tiled=True, axis_index_groups=[order]
    )

    owner = token_owners(context_lens, block_table, pages, page_size)
    scale = dim ** (-0.5)
    mixed = attend(query, owner, pool.reshape(pages * page_size, width), scale)
    returned = return_heads(mixed, me)
    attended = add_new_token(returned, queries, new_kv, dim, scale)

    slot = jnp.arange(slots, dtype=jnp.int32)
    per_peer = slots // peers
    where_from = place_of(slot // per_peer) * per_peer + slot % per_peer
    source = jnp.sum(
        jnp.where(recv_table[0][None, :] == slot[:, None], where_from[None, :], 0), axis=1
    )
    mixed, recv_pool = lax.optimization_barrier((mixed, recv_pool))
    old = stage(recv_pool.reshape(slots, page_size, width))
    landed = land_pages(arrived, old, source)
    return (attended, landed.reshape(recv_pool.shape))


def solution(mesh):
    return jax.shard_map(
        on_device,
        mesh=mesh,
        in_specs=(
            P(("inst", "tp"), None),
            P(("inst", "tp"), None),
            P("inst", None, None, "tp", None),
            P("inst"),
            P("inst", None),
            P("inst", None),
            P("inst", None),
            P("inst", None, None, "tp", None),
            P("inst", None),
        ),
        out_specs=(P(("inst", "tp"), None), P("inst", None, None, "tp", None)),
        check_vma=False,
    )
```

```python
import functools

import jax
import jax.numpy as jnp
from jax import lax
from jax.experimental import pallas as pl
from jax.experimental.pallas import tpu as pltpu
from jax.sharding import PartitionSpec as P

EMPTY = 256.0
EDGE = 64.0
MASKED = -1e30
LEVEL_PARTS = 3


def place_of(inst):
    x, z, half = inst >> 4, (inst >> 1) & 7, inst & 1
    return (1 - half) * 32 + (7 - z) * 4 + x


def pack_kernel(capacity, pages_ref, dest_ref, pool_ref, out_ref, pages, dest, taken, packed, sems):
    listed = dest.shape[1]
    peers = taken.shape[0]
    lists = (
        pltpu.make_async_copy(pages_ref, pages, sems.at[0]),
        pltpu.make_async_copy(dest_ref, dest, sems.at[1]),
    )
    for copy in lists:
        copy.start()
    packed[...] = jnp.full(packed.shape, EMPTY, packed.dtype)

    def clear(peer, carry):
        taken[peer] = 0
        return carry

    lax.fori_loop(0, peers, clear, 0, unroll=8)
    for copy in lists:
        copy.wait()

    def send(index, carry):
        peer = dest[0, index]
        position = taken[peer]
        taken[peer] = position + 1
        pltpu.make_async_copy(
            pool_ref.at[pages[0, index]],
            packed.at[place_of(peer) * capacity + position],
            sems.at[2],
        ).start()
        return carry

    lax.fori_loop(0, listed, send, 0, unroll=8)
    pltpu.make_async_copy(
        pool_ref.at[pl.ds(0, listed)], packed.at[pl.ds(0, listed)], sems.at[2]
    ).wait()
    done = pltpu.make_async_copy(packed, out_ref, sems.at[0])
    done.start()
    done.wait()


def pack_pages(pool, pages, dest, peers, capacity):
    page_shape = pool.shape[1:]
    listed = dest.shape[1]
    packed_shape = (peers * capacity,) + page_shape
    return pl.pallas_call(
        functools.partial(pack_kernel, capacity),
        out_shape=jax.ShapeDtypeStruct(packed_shape, pool.dtype),
        in_specs=[
            pl.BlockSpec(memory_space=pl.ANY),
            pl.BlockSpec(memory_space=pl.ANY),
            pl.BlockSpec(memory_space=pltpu.HBM),
        ],
        out_specs=pl.BlockSpec(memory_space=pl.ANY),
        scratch_shapes=[
            pltpu.SMEM((1, listed), jnp.int32),
            pltpu.SMEM((1, listed), jnp.int32),
            pltpu.SMEM((peers,), jnp.int32),
            pltpu.VMEM(packed_shape, pool.dtype),
            pltpu.SemaphoreType.DMA((3,)),
        ],
        name="pack_pages",
    )(pages, dest, pool)


def stage_kernel(from_ref, to_ref, sem):
    copy = pltpu.make_async_copy(from_ref, to_ref, sem)
    copy.start()
    copy.wait()


def stage(x):
    return pl.pallas_call(
        stage_kernel,
        out_shape=pltpu.VMEM(x.shape, x.dtype),
        in_specs=[pl.BlockSpec(memory_space=pltpu.HBM)],
        out_specs=pl.BlockSpec(memory_space=pltpu.VMEM),
        scratch_shapes=[pltpu.SemaphoreType.DMA],
        compiler_params=pltpu.CompilerParams(vmem_limit_bytes=16 * 1024 * 1024),
        name="stage_old_pages",
    )(x)


def land_kernel(source_ref, arrived_ref, old_ref, out_ref, landed, sems):
    slots = landed.shape[0]
    parts = sems.shape[0]
    step = slots // parts
    copies = []
    for part in range(parts):

        def place(slot, carry):
            page = arrived_ref[source_ref[slot]]
            landed[slot] = jnp.where(page > EDGE, old_ref[slot], page)
            return carry

        lax.fori_loop(part * step, (part + 1) * step, place, 0, unroll=True)
        copies.append(
            pltpu.make_async_copy(
                landed.at[pl.ds(part * step, step)],
                out_ref.at[pl.ds(part * step, step)],
                sems.at[part],
            )
        )
        copies[-1].start()
    for copy in copies:
        copy.wait()


def land_pages(arrived, old, source):
    return pl.pallas_call(
        land_kernel,
        out_shape=jax.ShapeDtypeStruct(old.shape, old.dtype),
        in_specs=[
            pl.BlockSpec(memory_space=pltpu.SMEM),
            pl.BlockSpec(memory_space=pltpu.VMEM),
            pl.BlockSpec(memory_space=pltpu.VMEM),
        ],
        out_specs=pl.BlockSpec(memory_space=pl.ANY),
        scratch_shapes=[
            pltpu.VMEM(old.shape, old.dtype),
            pltpu.SemaphoreType.DMA((8,)),
        ],
        compiler_params=pltpu.CompilerParams(vmem_limit_bytes=16 * 1024 * 1024),
        name="land_pages",
    )(source, arrived, old)


def attend_kernel(scale, query_ref, owner_ref, pool_ref, out_ref, score_ref):
    rows = query_ref.shape[0]
    dim = pool_ref.shape[1] // 2
    group = query_ref.shape[1] // dim
    lanes = owner_ref.shape[1]
    chunk = 4 * lanes
    tokens = pool_ref.shape[0]
    query = jnp.concatenate([query_ref[:, j * dim : (j + 1) * dim] for j in range(group)], axis=0)
    row_of = lax.broadcasted_iota(jnp.int32, (group * rows, lanes), 0) % rows
    top = jnp.full((group * rows, lanes), MASKED, jnp.float32)
    for start in range(0, tokens, chunk):
        keys = pool_ref[start : start + chunk, :dim]
        scores = (
            lax.dot_general(
                query, keys, (((1,), (1,)), ((), ())), preferred_element_type=jnp.float32
            )
            * scale
        )
        for part in range(chunk // lanes):
            block = start // lanes + part
            kept = jnp.where(
                owner_ref[block : block + 1, :] == row_of,
                scores[:, part * lanes : (part + 1) * lanes],
                MASKED,
            )
            score_ref[:, block * lanes : (block + 1) * lanes] = kept
            top = jnp.maximum(top, kept)
    top = jnp.max(top, axis=1, keepdims=True)
    total = jnp.zeros((group * rows, lanes), jnp.float32)
    mixed = jnp.zeros((group * rows, dim), jnp.float32)
    for start in range(0, tokens, chunk):
        weights = jnp.exp(score_ref[:, start : start + chunk] - top)
        for part in range(chunk // lanes):
            total = total + weights[:, part * lanes : (part + 1) * lanes]
        mixed = mixed + jnp.dot(
            weights.astype(jnp.bfloat16),
            pool_ref[start : start + chunk, dim:],
            preferred_element_type=jnp.float32,
        )
    total = jnp.sum(total, axis=1, keepdims=True)
    mixed = (mixed / total).astype(out_ref.dtype)
    level = top + jnp.log(total)
    lane = lax.broadcasted_iota(jnp.int32, (rows, lanes), 1)
    levels = jnp.zeros((rows, lanes), jnp.float32)
    for j in range(group):
        out_ref[:, j * dim : (j + 1) * dim] = mixed[j * rows : (j + 1) * rows]
        rest = level[j * rows : (j + 1) * rows]
        for part in range(LEVEL_PARTS):
            piece = rest.astype(out_ref.dtype).astype(jnp.float32)
            levels = jnp.where(lane == part * group + j, piece, levels)
            rest = rest - piece
    out_ref[:, group * dim :] = levels.astype(out_ref.dtype)


def attend(query, owner, pool, scale):
    rows, dim = query.shape[0], pool.shape[1] // 2
    group = query.shape[1] // dim
    tokens = pool.shape[0]
    return pl.pallas_call(
        functools.partial(attend_kernel, scale),
        out_shape=jax.ShapeDtypeStruct((rows, group * dim + 128), query.dtype),
        in_specs=[pl.BlockSpec(memory_space=pltpu.VMEM)] * 3,
        out_specs=pl.BlockSpec(memory_space=pltpu.VMEM),
        scratch_shapes=[pltpu.VMEM((rows * group, tokens), jnp.float32)],
        compiler_params=pltpu.CompilerParams(vmem_limit_bytes=24 * 1024 * 1024),
        cost_estimate=pl.CostEstimate(
            flops=4 * rows * group * tokens * dim,
            bytes_accessed=pool.size * 2,
            transcendentals=rows * group * tokens,
        ),
        name="attend",
    )(query, owner, pool)


def token_owners(lengths, table, pages, page_size):
    rows, per_row = table.shape
    block = jnp.arange(rows * per_row, dtype=jnp.int32)
    row = block // per_row
    live = jnp.clip(
        (lengths[:, None] - jnp.arange(per_row, dtype=jnp.int32)[None, :] * page_size),
        0,
        page_size,
    ).reshape(-1)
    coded = row * (2 * page_size) + live
    page = jnp.arange(pages, dtype=jnp.int32)
    of_page = jnp.sum(
        jnp.where(table.reshape(-1)[None, :] == page[:, None], coded[None, :], 0), axis=1
    )
    per_line = 128 // page_size
    offset = jnp.arange(page_size, dtype=jnp.int32)
    of_page = of_page.reshape(pages // per_line, per_line, 1)
    owner = jnp.where(offset < of_page % (2 * page_size), of_page // (2 * page_size), -1)
    return owner.reshape(pages // per_line, 128)


def pair_gather(x):
    groups = lax.axis_size("tp")
    chips = [[2 * i, 2 * i + 1] for i in range(groups // 2)]
    return lax.all_gather(x, "tp", axis=0, tiled=False, axis_index_groups=chips)


def chip_exchange(pieces):
    groups = lax.axis_size("tp")
    chip = lax.axis_index("tp") // 2
    chips = pieces.shape[0]
    got = [lax.dynamic_index_in_dim(pieces, chip, 0, keepdims=False)]
    for k in range(1, chips):
        piece = lax.dynamic_index_in_dim(pieces, chip ^ k, 0, keepdims=False)
        got.append(lax.ppermute(piece, "tp", [(i, i ^ (2 * k)) for i in range(groups)]))
    return got


def gather_queries(queries):
    groups = lax.axis_size("tp")
    rows = queries.shape[0]
    split = queries.reshape(rows, groups, -1)
    got = lax.all_to_all(split, "tp", split_axis=1, concat_axis=0, tiled=True)
    return got.reshape(groups * rows, -1)


def return_heads(mixed, me):
    groups = lax.axis_size("tp")
    rows, width = mixed.shape
    rows_local = rows // groups
    both = pair_gather(mixed)
    both = both.reshape(2, groups // 2, 2, rows_local, width)
    mine = lax.dynamic_index_in_dim(both, me % 2, 2, keepdims=False)
    return chip_exchange(mine.transpose(1, 0, 2, 3))


def add_new_kernel(dim, scale, chip_ref, query_ref, fresh_ref, *refs):
    pieces, out_ref = refs[:-1], refs[-1]
    heads, _, width = pieces[0].shape
    lanes = 128
    group = (width - lanes) // dim
    chip = chip_ref[0]
    lane = lax.broadcasted_iota(jnp.int32, (pieces[0].shape[1], lanes), 1)
    results = []
    for k, piece in enumerate(pieces):
        for h in range(heads):
            place = (chip ^ k) * heads + h
            fresh = pl.multiple_of(place * (2 * dim), 2 * dim)
            fresh_key = fresh_ref[:, pl.ds(fresh, dim)].astype(jnp.float32)
            fresh_value = fresh_ref[:, pl.ds(fresh + dim, dim)].astype(jnp.float32)
            parts = piece[h, :, group * dim :].astype(jnp.float32)
            level = parts
            for part in range(1, LEVEL_PARTS):
                level = level + pltpu.roll(parts, lanes - part * group, 1)
            own = jnp.zeros_like(level)
            places = []
            for j in range(group):
                places.append(pl.multiple_of(place * (group * dim) + j * dim, dim))
                query = query_ref[:, pl.ds(places[-1], dim)].astype(jnp.float32)
                score = jnp.sum(query * fresh_key, axis=1, keepdims=True) * scale
                own = jnp.where(lane == j, score, own)
            top = jnp.maximum(level, own)
            cached, new = jnp.exp(level - top), jnp.exp(own - top)
            total = cached + new
            cached, new = cached / total, new / total
            for j in range(group):
                value = piece[h, :, j * dim : (j + 1) * dim].astype(jnp.float32)
                mixed = value * cached[:, j : j + 1] + fresh_value * new[:, j : j + 1]
                results.append((places[j], mixed.astype(out_ref.dtype)))
    for at, mixed in results:
        out_ref[:, pl.ds(at, dim)] = mixed


def add_new_token(pieces, queries, new_kv, dim, scale):
    chip = (lax.axis_index("tp") // 2).astype(jnp.int32).reshape(1)
    vmem = pl.BlockSpec(memory_space=pltpu.VMEM)
    return pl.pallas_call(
        functools.partial(add_new_kernel, dim, scale),
        out_shape=jax.ShapeDtypeStruct(queries.shape, queries.dtype),
        in_specs=[pl.BlockSpec(memory_space=pltpu.SMEM)] + [vmem] * (2 + len(pieces)),
        out_specs=vmem,
        compiler_params=pltpu.CompilerParams(vmem_limit_bytes=16 * 1024 * 1024),
        cost_estimate=pl.CostEstimate(
            flops=8 * queries.size,
            bytes_accessed=4 * queries.size,
            transcendentals=2 * queries.size // dim,
        ),
        name="add_new_token",
    )(chip, queries, new_kv, *pieces)


def on_device(
    queries,
    new_kv,
    kv_pool,
    context_lens,
    block_table,
    send_pages,
    send_dest,
    recv_pool,
    recv_table,
):
    peers = lax.axis_size("inst")
    me = lax.axis_index("tp")
    _, pages, page_size, kv_local, width = kv_pool.shape
    dim = width // 2
    slots = recv_table.shape[1]
    pool = kv_pool.reshape(pages, page_size, width)

    query = gather_queries(queries)
    outgoing = pack_pages(pool, send_pages, send_dest.reshape(1, -1), peers, slots // peers)
    query, outgoing = lax.optimization_barrier((query, outgoing))
    order = sorted(range(peers), key=place_of)
    arrived = lax.all_to_all(
        outgoing, "inst", split_axis=0, concat_axis=0, tiled=True, axis_index_groups=[order]
    )

    owner = token_owners(context_lens, block_table, pages, page_size)
    scale = dim ** (-0.5)
    mixed = attend(query, owner, pool.reshape(pages * page_size, width), scale)
    returned = return_heads(mixed, me)
    attended = add_new_token(returned, queries, new_kv, dim, scale)

    slot = jnp.arange(slots, dtype=jnp.int32)
    per_peer = slots // peers
    where_from = place_of(slot // per_peer) * per_peer + slot % per_peer
    source = jnp.sum(
        jnp.where(recv_table[0][None, :] == slot[:, None], where_from[None, :], 0), axis=1
    )
    mixed, recv_pool = lax.optimization_barrier((mixed, recv_pool))
    old = stage(recv_pool.reshape(slots, page_size, width))
    landed = land_pages(arrived, old, source)
    return (attended, landed.reshape(recv_pool.shape))


def solution(mesh):
    return jax.shard_map(
        on_device,
        mesh=mesh,
        in_specs=(
            P(("inst", "tp"), None),
            P(("inst", "tp"), None),
            P("inst", None, None, "tp", None),
            P("inst"),
            P("inst", None),
            P("inst", None),
            P("inst", None),
            P("inst", None, None, "tp", None),
            P("inst", None),
        ),
        out_specs=(P(("inst", "tp"), None), P("inst", None, None, "tp", None)),
        check_vma=False,
    )
```

```python
import functools

import jax
import jax.numpy as jnp
from jax import lax
from jax.experimental import pallas as pl
from jax.experimental.pallas import tpu as pltpu
from jax.sharding import PartitionSpec as P

EMPTY = 256.0
EDGE = 64.0
MASKED = -1e30
LEVEL_PARTS = 3


def place_of(inst):
    x, z, half = inst >> 4, (inst >> 1) & 7, inst & 1
    return (1 - half) * 32 + (7 - z) * 4 + x


def pack_kernel(capacity, pages_ref, dest_ref, pool_ref, out_ref, pages, dest, taken, packed, sems):
    listed = dest.shape[1]
    peers = taken.shape[0]
    lists = (
        pltpu.make_async_copy(pages_ref, pages, sems.at[0]),
        pltpu.make_async_copy(dest_ref, dest, sems.at[1]),
    )
    for copy in lists:
        copy.start()
    packed[...] = jnp.full(packed.shape, EMPTY, packed.dtype)

    def clear(peer, carry):
        taken[peer] = 0
        return carry

    lax.fori_loop(0, peers, clear, 0, unroll=8)
    for copy in lists:
        copy.wait()

    def send(index, carry):
        peer = dest[0, index]
        position = taken[peer]
        taken[peer] = position + 1
        pltpu.make_async_copy(
            pool_ref.at[pages[0, index]],
            packed.at[place_of(peer) * capacity + position],
            sems.at[2],
        ).start()
        return carry

    lax.fori_loop(0, listed, send, 0, unroll=8)
    pltpu.make_async_copy(
        pool_ref.at[pl.ds(0, listed)], packed.at[pl.ds(0, listed)], sems.at[2]
    ).wait()
    done = pltpu.make_async_copy(packed, out_ref, sems.at[0])
    done.start()
    done.wait()


def pack_pages(pool, pages, dest, peers, capacity):
    page_shape = pool.shape[1:]
    listed = dest.shape[1]
    packed_shape = (peers * capacity,) + page_shape
    return pl.pallas_call(
        functools.partial(pack_kernel, capacity),
        out_shape=jax.ShapeDtypeStruct(packed_shape, pool.dtype),
        in_specs=[
            pl.BlockSpec(memory_space=pl.ANY),
            pl.BlockSpec(memory_space=pl.ANY),
            pl.BlockSpec(memory_space=pltpu.HBM),
        ],
        out_specs=pl.BlockSpec(memory_space=pl.ANY),
        scratch_shapes=[
            pltpu.SMEM((1, listed), jnp.int32),
            pltpu.SMEM((1, listed), jnp.int32),
            pltpu.SMEM((peers,), jnp.int32),
            pltpu.VMEM(packed_shape, pool.dtype),
            pltpu.SemaphoreType.DMA((3,)),
        ],
        name="pack_pages",
    )(pages, dest, pool)


def stage_kernel(from_ref, to_ref, sem):
    copy = pltpu.make_async_copy(from_ref, to_ref, sem)
    copy.start()
    copy.wait()


def stage(x):
    return pl.pallas_call(
        stage_kernel,
        out_shape=pltpu.VMEM(x.shape, x.dtype),
        in_specs=[pl.BlockSpec(memory_space=pltpu.HBM)],
        out_specs=pl.BlockSpec(memory_space=pltpu.VMEM),
        scratch_shapes=[pltpu.SemaphoreType.DMA],
        compiler_params=pltpu.CompilerParams(vmem_limit_bytes=16 * 1024 * 1024),
        name="stage_old_pages",
    )(x)


def land_kernel(source_ref, arrived_ref, old_ref, out_ref, landed, sems):
    slots = landed.shape[0]
    parts = sems.shape[0]
    step = slots // parts
    copies = []
    for part in range(parts):

        def place(slot, carry):
            page = arrived_ref[source_ref[slot]]
            landed[slot] = jnp.where(page > EDGE, old_ref[slot], page)
            return carry

        lax.fori_loop(part * step, (part + 1) * step, place, 0, unroll=True)
        copies.append(
            pltpu.make_async_copy(
                landed.at[pl.ds(part * step, step)],
                out_ref.at[pl.ds(part * step, step)],
                sems.at[part],
            )
        )
        copies[-1].start()
    for copy in copies:
        copy.wait()


def land_pages(arrived, old, source):
    return pl.pallas_call(
        land_kernel,
        out_shape=jax.ShapeDtypeStruct(old.shape, old.dtype),
        in_specs=[
            pl.BlockSpec(memory_space=pltpu.SMEM),
            pl.BlockSpec(memory_space=pltpu.VMEM),
            pl.BlockSpec(memory_space=pltpu.VMEM),
        ],
        out_specs=pl.BlockSpec(memory_space=pl.ANY),
        scratch_shapes=[
            pltpu.VMEM(old.shape, old.dtype),
            pltpu.SemaphoreType.DMA((8,)),
        ],
        compiler_params=pltpu.CompilerParams(vmem_limit_bytes=16 * 1024 * 1024),
        name="land_pages",
    )(source, arrived, old)


def attend_kernel(scale, query_ref, owner_ref, pool_ref, out_ref, score_ref):
    rows = query_ref.shape[0]
    dim = pool_ref.shape[1] // 2
    group = query_ref.shape[1] // dim
    lanes = owner_ref.shape[1]
    chunk = 4 * lanes
    tokens = pool_ref.shape[0]
    query = jnp.concatenate([query_ref[:, j * dim : (j + 1) * dim] for j in range(group)], axis=0)
    row_of = lax.broadcasted_iota(jnp.int32, (group * rows, lanes), 0) % rows
    top = jnp.full((group * rows, lanes), MASKED, jnp.float32)
    for start in range(0, tokens, chunk):
        keys = pool_ref[start : start + chunk, :dim]
        scores = (
            lax.dot_general(
                query, keys, (((1,), (1,)), ((), ())), preferred_element_type=jnp.float32
            )
            * scale
        )
        for part in range(chunk // lanes):
            block = start // lanes + part
            kept = jnp.where(
                owner_ref[block : block + 1, :] == row_of,
                scores[:, part * lanes : (part + 1) * lanes],
                MASKED,
            )
            score_ref[:, block * lanes : (block + 1) * lanes] = kept
            top = jnp.maximum(top, kept)
    top = jnp.max(top, axis=1, keepdims=True)
    total = jnp.zeros((group * rows, lanes), jnp.float32)
    mixed = jnp.zeros((group * rows, dim), jnp.float32)
    for start in range(0, tokens, chunk):
        weights = jnp.exp(score_ref[:, start : start + chunk] - top)
        for part in range(chunk // lanes):
            total = total + weights[:, part * lanes : (part + 1) * lanes]
        mixed = mixed + jnp.dot(
            weights.astype(jnp.bfloat16),
            pool_ref[start : start + chunk, dim:],
            preferred_element_type=jnp.float32,
        )
    total = jnp.sum(total, axis=1, keepdims=True)
    mixed = (mixed / total).astype(out_ref.dtype)
    level = top + jnp.log(total)
    lane = lax.broadcasted_iota(jnp.int32, (rows, lanes), 1)
    levels = jnp.zeros((rows, lanes), jnp.float32)
    for j in range(group):
        out_ref[:, j * dim : (j + 1) * dim] = mixed[j * rows : (j + 1) * rows]
        rest = level[j * rows : (j + 1) * rows]
        for part in range(LEVEL_PARTS):
            piece = rest.astype(out_ref.dtype).astype(jnp.float32)
            levels = jnp.where(lane == part * group + j, piece, levels)
            rest = rest - piece
    out_ref[:, group * dim :] = levels.astype(out_ref.dtype)


def attend(query, owner, pool, scale):
    rows, dim = query.shape[0], pool.shape[1] // 2
    group = query.shape[1] // dim
    tokens = pool.shape[0]
    return pl.pallas_call(
        functools.partial(attend_kernel, scale),
        out_shape=jax.ShapeDtypeStruct((rows, group * dim + 128), query.dtype),
        in_specs=[pl.BlockSpec(memory_space=pltpu.VMEM)] * 3,
        out_specs=pl.BlockSpec(memory_space=pltpu.VMEM),
        scratch_shapes=[pltpu.VMEM((rows * group, tokens), jnp.float32)],
        compiler_params=pltpu.CompilerParams(vmem_limit_bytes=24 * 1024 * 1024),
        cost_estimate=pl.CostEstimate(
            flops=4 * rows * group * tokens * dim,
            bytes_accessed=pool.size * 2,
            transcendentals=rows * group * tokens,
        ),
        name="attend",
    )(query, owner, pool)


def token_owners(lengths, table, pages, page_size):
    rows, per_row = table.shape
    block = jnp.arange(rows * per_row, dtype=jnp.int32)
    row = block // per_row
    live = jnp.clip(
        (lengths[:, None] - jnp.arange(per_row, dtype=jnp.int32)[None, :] * page_size),
        0,
        page_size,
    ).reshape(-1)
    coded = row * (2 * page_size) + live
    page = jnp.arange(pages, dtype=jnp.int32)
    of_page = jnp.sum(
        jnp.where(table.reshape(-1)[None, :] == page[:, None], coded[None, :], 0), axis=1
    )
    per_line = 128 // page_size
    offset = jnp.arange(page_size, dtype=jnp.int32)
    of_page = of_page.reshape(pages // per_line, per_line, 1)
    owner = jnp.where(offset < of_page % (2 * page_size), of_page // (2 * page_size), -1)
    return owner.reshape(pages // per_line, 128)


def pair_gather(x):
    groups = lax.axis_size("tp")
    chips = [[2 * i, 2 * i + 1] for i in range(groups // 2)]
    return lax.all_gather(x, "tp", axis=0, tiled=False, axis_index_groups=chips)


def chip_exchange(pieces):
    groups = lax.axis_size("tp")
    chip = lax.axis_index("tp") // 2
    chips = pieces.shape[0]
    got = [lax.dynamic_index_in_dim(pieces, chip, 0, keepdims=False)]
    for k in range(1, chips):
        piece = lax.dynamic_index_in_dim(pieces, chip ^ k, 0, keepdims=False)
        got.append(lax.ppermute(piece, "tp", [(i, i ^ (2 * k)) for i in range(groups)]))
    return got


def gather_queries(queries):
    groups = lax.axis_size("tp")
    rows = queries.shape[0]
    split = queries.reshape(rows, groups // 2, -1)
    got = lax.all_to_all(
        split,
        "tp",
        split_axis=1,
        concat_axis=0,
        tiled=True,
        axis_index_groups=[[i for i in range(groups) if i % 2 == core] for core in (0, 1)],
    )
    return got.reshape(groups // 2 * rows, -1)


def share_queries(part, rows_local, me):
    rows, width = part.shape
    both = pair_gather(part).reshape(2, rows // rows_local, rows_local, 2, width // 2)
    mine = lax.dynamic_index_in_dim(both, me % 2, 3, keepdims=False)
    return mine.transpose(1, 0, 2, 3).reshape(2 * rows, width // 2)


def return_heads(mixed, me):
    groups = lax.axis_size("tp")
    rows, width = mixed.shape
    rows_local = rows // groups
    both = pair_gather(mixed)
    both = both.reshape(2, groups // 2, 2, rows_local, width)
    mine = lax.dynamic_index_in_dim(both, me % 2, 2, keepdims=False)
    return chip_exchange(mine.transpose(1, 0, 2, 3))


def add_new_kernel(dim, scale, chip_ref, query_ref, fresh_ref, *refs):
    pieces, out_ref = refs[:-1], refs[-1]
    heads, _, width = pieces[0].shape
    lanes = 128
    group = (width - lanes) // dim
    chip = chip_ref[0]
    lane = lax.broadcasted_iota(jnp.int32, (pieces[0].shape[1], lanes), 1)
    results = []
    for k, piece in enumerate(pieces):
        for h in range(heads):
            place = (chip ^ k) * heads + h
            fresh = pl.multiple_of(place * (2 * dim), 2 * dim)
            fresh_key = fresh_ref[:, pl.ds(fresh, dim)].astype(jnp.float32)
            fresh_value = fresh_ref[:, pl.ds(fresh + dim, dim)].astype(jnp.float32)
            parts = piece[h, :, group * dim :].astype(jnp.float32)
            level = parts
            for part in range(1, LEVEL_PARTS):
                level = level + pltpu.roll(parts, lanes - part * group, 1)
            own = jnp.zeros_like(level)
            places = []
            for j in range(group):
                places.append(pl.multiple_of(place * (group * dim) + j * dim, dim))
                query = query_ref[:, pl.ds(places[-1], dim)].astype(jnp.float32)
                score = jnp.sum(query * fresh_key, axis=1, keepdims=True) * scale
                own = jnp.where(lane == j, score, own)
            top = jnp.maximum(level, own)
            cached, new = jnp.exp(level - top), jnp.exp(own - top)
            total = cached + new
            cached, new = cached / total, new / total
            for j in range(group):
                value = piece[h, :, j * dim : (j + 1) * dim].astype(jnp.float32)
                mixed = value * cached[:, j : j + 1] + fresh_value * new[:, j : j + 1]
                results.append((places[j], mixed.astype(out_ref.dtype)))
    for at, mixed in results:
        out_ref[:, pl.ds(at, dim)] = mixed


def add_new_token(pieces, queries, new_kv, dim, scale):
    chip = (lax.axis_index("tp") // 2).astype(jnp.int32).reshape(1)
    vmem = pl.BlockSpec(memory_space=pltpu.VMEM)
    return pl.pallas_call(
        functools.partial(add_new_kernel, dim, scale),
        out_shape=jax.ShapeDtypeStruct(queries.shape, queries.dtype),
        in_specs=[pl.BlockSpec(memory_space=pltpu.SMEM)] + [vmem] * (2 + len(pieces)),
        out_specs=vmem,
        compiler_params=pltpu.CompilerParams(vmem_limit_bytes=16 * 1024 * 1024),
        cost_estimate=pl.CostEstimate(
            flops=8 * queries.size,
            bytes_accessed=4 * queries.size,
            transcendentals=2 * queries.size // dim,
        ),
        name="add_new_token",
    )(chip, queries, new_kv, *pieces)


def on_device(
    queries,
    new_kv,
    kv_pool,
    context_lens,
    block_table,
    send_pages,
    send_dest,
    recv_pool,
    recv_table,
):
    peers = lax.axis_size("inst")
    me = lax.axis_index("tp")
    _, pages, page_size, kv_local, width = kv_pool.shape
    dim = width // 2
    slots = recv_table.shape[1]
    pool = kv_pool.reshape(pages, page_size, width)

    query = gather_queries(queries)
    outgoing = pack_pages(pool, send_pages, send_dest.reshape(1, -1), peers, slots // peers)
    query, outgoing = lax.optimization_barrier((query, outgoing))
    order = sorted(range(peers), key=place_of)
    arrived = lax.all_to_all(
        outgoing, "inst", split_axis=0, concat_axis=0, tiled=True, axis_index_groups=[order]
    )

    owner = token_owners(context_lens, block_table, pages, page_size)
    scale = dim ** (-0.5)
    query = share_queries(query, queries.shape[0], me)
    mixed = attend(query, owner, pool.reshape(pages * page_size, width), scale)
    returned = return_heads(mixed, me)
    attended = add_new_token(returned, queries, new_kv, dim, scale)

    slot = jnp.arange(slots, dtype=jnp.int32)
    per_peer = slots // peers
    where_from = place_of(slot // per_peer) * per_peer + slot % per_peer
    source = jnp.sum(
        jnp.where(recv_table[0][None, :] == slot[:, None], where_from[None, :], 0), axis=1
    )
    mixed, recv_pool = lax.optimization_barrier((mixed, recv_pool))
    old = stage(recv_pool.reshape(slots, page_size, width))
    landed = land_pages(arrived, old, source)
    return (attended, landed.reshape(recv_pool.shape))


def solution(mesh):
    return jax.shard_map(
        on_device,
        mesh=mesh,
        in_specs=(
            P(("inst", "tp"), None),
            P(("inst", "tp"), None),
            P("inst", None, None, "tp", None),
            P("inst"),
            P("inst", None),
            P("inst", None),
            P("inst", None),
            P("inst", None, None, "tp", None),
            P("inst", None),
        ),
        out_specs=(P(("inst", "tp"), None), P("inst", None, None, "tp", None)),
        check_vma=False,
    )
```

```python
import functools

import jax
import jax.numpy as jnp
from jax import lax
from jax.experimental import pallas as pl
from jax.experimental.pallas import tpu as pltpu
from jax.sharding import PartitionSpec as P

EMPTY = 256.0
EDGE = 64.0
MASKED = -1e30
LEVEL_PARTS = 3


def place_of(inst):
    x, z, half = inst >> 4, (inst >> 1) & 7, inst & 1
    return (1 - half) * 32 + (7 - z) * 4 + x


def pack_kernel(capacity, pages_ref, dest_ref, pool_ref, out_ref, pages, dest, taken, packed, sems):
    listed = dest.shape[1]
    peers = taken.shape[0]
    lists = (
        pltpu.make_async_copy(pages_ref, pages, sems.at[0]),
        pltpu.make_async_copy(dest_ref, dest, sems.at[1]),
    )
    for copy in lists:
        copy.start()
    packed[...] = jnp.full(packed.shape, EMPTY, packed.dtype)

    def clear(peer, carry):
        taken[peer] = 0
        return carry

    lax.fori_loop(0, peers, clear, 0, unroll=8)
    for copy in lists:
        copy.wait()

    def send(index, carry):
        peer = dest[0, index]
        position = taken[peer]
        taken[peer] = position + 1
        pltpu.make_async_copy(
            pool_ref.at[pages[0, index]],
            packed.at[place_of(peer) * capacity + position],
            sems.at[2],
        ).start()
        return carry

    lax.fori_loop(0, listed, send, 0, unroll=8)
    pltpu.make_async_copy(
        pool_ref.at[pl.ds(0, listed)], packed.at[pl.ds(0, listed)], sems.at[2]
    ).wait()
    done = pltpu.make_async_copy(packed, out_ref, sems.at[0])
    done.start()
    done.wait()


def pack_pages(pool, pages, dest, peers, capacity):
    page_shape = pool.shape[1:]
    listed = dest.shape[1]
    packed_shape = (peers * capacity,) + page_shape
    return pl.pallas_call(
        functools.partial(pack_kernel, capacity),
        out_shape=jax.ShapeDtypeStruct(packed_shape, pool.dtype),
        in_specs=[
            pl.BlockSpec(memory_space=pl.ANY),
            pl.BlockSpec(memory_space=pl.ANY),
            pl.BlockSpec(memory_space=pltpu.HBM),
        ],
        out_specs=pl.BlockSpec(memory_space=pl.ANY),
        scratch_shapes=[
            pltpu.SMEM((1, listed), jnp.int32),
            pltpu.SMEM((1, listed), jnp.int32),
            pltpu.SMEM((peers,), jnp.int32),
            pltpu.VMEM(packed_shape, pool.dtype),
            pltpu.SemaphoreType.DMA((3,)),
        ],
        name="pack_pages",
    )(pages, dest, pool)


def stage_kernel(from_ref, to_ref, sem):
    copy = pltpu.make_async_copy(from_ref, to_ref, sem)
    copy.start()
    copy.wait()


def stage(x):
    return pl.pallas_call(
        stage_kernel,
        out_shape=pltpu.VMEM(x.shape, x.dtype),
        in_specs=[pl.BlockSpec(memory_space=pltpu.HBM)],
        out_specs=pl.BlockSpec(memory_space=pltpu.VMEM),
        scratch_shapes=[pltpu.SemaphoreType.DMA],
        compiler_params=pltpu.CompilerParams(vmem_limit_bytes=16 * 1024 * 1024),
        name="stage_old_pages",
    )(x)


def land_kernel(source_ref, arrived_ref, old_ref, out_ref, landed, sems):
    slots = landed.shape[0]
    parts = sems.shape[0]
    step = slots // parts
    copies = []
    for part in range(parts):

        def place(slot, carry):
            page = arrived_ref[source_ref[slot]]
            landed[slot] = jnp.where(page > EDGE, old_ref[slot], page)
            return carry

        lax.fori_loop(part * step, (part + 1) * step, place, 0, unroll=True)
        copies.append(
            pltpu.make_async_copy(
                landed.at[pl.ds(part * step, step)],
                out_ref.at[pl.ds(part * step, step)],
                sems.at[part],
            )
        )
        copies[-1].start()
    for copy in copies:
        copy.wait()


def land_pages(arrived, old, source):
    return pl.pallas_call(
        land_kernel,
        out_shape=jax.ShapeDtypeStruct(old.shape, old.dtype),
        in_specs=[
            pl.BlockSpec(memory_space=pltpu.SMEM),
            pl.BlockSpec(memory_space=pltpu.VMEM),
            pl.BlockSpec(memory_space=pltpu.VMEM),
        ],
        out_specs=pl.BlockSpec(memory_space=pl.ANY),
        scratch_shapes=[
            pltpu.VMEM(old.shape, old.dtype),
            pltpu.SemaphoreType.DMA((4,)),
        ],
        compiler_params=pltpu.CompilerParams(vmem_limit_bytes=16 * 1024 * 1024),
        name="land_pages",
    )(source, arrived, old)


def attend_kernel(scale, query_ref, owner_ref, pool_ref, out_ref, score_ref):
    rows = query_ref.shape[0]
    dim = pool_ref.shape[1] // 2
    group = query_ref.shape[1] // dim
    lanes = owner_ref.shape[1]
    chunk = 4 * lanes
    tokens = pool_ref.shape[0]
    query = jnp.concatenate([query_ref[:, j * dim : (j + 1) * dim] for j in range(group)], axis=0)
    row_of = lax.broadcasted_iota(jnp.int32, (group * rows, lanes), 0) % rows
    top = jnp.full((group * rows, lanes), MASKED, jnp.float32)
    for start in range(0, tokens, chunk):
        keys = pool_ref[start : start + chunk, :dim]
        scores = (
            lax.dot_general(
                query, keys, (((1,), (1,)), ((), ())), preferred_element_type=jnp.float32
            )
            * scale
        )
        for part in range(chunk // lanes):
            block = start // lanes + part
            kept = jnp.where(
                owner_ref[block : block + 1, :] == row_of,
                scores[:, part * lanes : (part + 1) * lanes],
                MASKED,
            )
            score_ref[:, block * lanes : (block + 1) * lanes] = kept
            top = jnp.maximum(top, kept)
    top = jnp.max(top, axis=1, keepdims=True)
    total = jnp.zeros((group * rows, lanes), jnp.float32)
    mixed = jnp.zeros((group * rows, dim), jnp.float32)
    for start in range(0, tokens, chunk):
        weights = jnp.exp(score_ref[:, start : start + chunk] - top)
        for part in range(chunk // lanes):
            total = total + weights[:, part * lanes : (part + 1) * lanes]
        mixed = mixed + jnp.dot(
            weights.astype(jnp.bfloat16),
            pool_ref[start : start + chunk, dim:],
            preferred_element_type=jnp.float32,
        )
    total = jnp.sum(total, axis=1, keepdims=True)
    mixed = (mixed / total).astype(out_ref.dtype)
    level = top + jnp.log(total)
    lane = lax.broadcasted_iota(jnp.int32, (rows, lanes), 1)
    levels = jnp.zeros((rows, lanes), jnp.float32)
    for j in range(group):
        out_ref[:, j * dim : (j + 1) * dim] = mixed[j * rows : (j + 1) * rows]
        rest = level[j * rows : (j + 1) * rows]
        for part in range(LEVEL_PARTS):
            piece = rest.astype(out_ref.dtype).astype(jnp.float32)
            levels = jnp.where(lane == part * group + j, piece, levels)
            rest = rest - piece
    out_ref[:, group * dim :] = levels.astype(out_ref.dtype)


def attend(query, owner, pool, scale):
    rows, dim = query.shape[0], pool.shape[1] // 2
    group = query.shape[1] // dim
    tokens = pool.shape[0]
    return pl.pallas_call(
        functools.partial(attend_kernel, scale),
        out_shape=jax.ShapeDtypeStruct((rows, group * dim + 128), query.dtype),
        in_specs=[pl.BlockSpec(memory_space=pltpu.VMEM)] * 3,
        out_specs=pl.BlockSpec(memory_space=pltpu.VMEM),
        scratch_shapes=[pltpu.VMEM((rows * group, tokens), jnp.float32)],
        compiler_params=pltpu.CompilerParams(vmem_limit_bytes=24 * 1024 * 1024),
        cost_estimate=pl.CostEstimate(
            flops=4 * rows * group * tokens * dim,
            bytes_accessed=pool.size * 2,
            transcendentals=rows * group * tokens,
        ),
        name="attend",
    )(query, owner, pool)


def token_owners(lengths, table, pages, page_size):
    rows, per_row = table.shape
    block = jnp.arange(rows * per_row, dtype=jnp.int32)
    row = block // per_row
    live = jnp.clip(
        (lengths[:, None] - jnp.arange(per_row, dtype=jnp.int32)[None, :] * page_size),
        0,
        page_size,
    ).reshape(-1)
    coded = row * (2 * page_size) + live
    page = jnp.arange(pages, dtype=jnp.int32)
    of_page = jnp.sum(
        jnp.where(table.reshape(-1)[None, :] == page[:, None], coded[None, :], 0), axis=1
    )
    per_line = 128 // page_size
    offset = jnp.arange(page_size, dtype=jnp.int32)
    of_page = of_page.reshape(pages // per_line, per_line, 1)
    owner = jnp.where(offset < of_page % (2 * page_size), of_page // (2 * page_size), -1)
    return owner.reshape(pages // per_line, 128)


def pair_gather(x):
    groups = lax.axis_size("tp")
    chips = [[2 * i, 2 * i + 1] for i in range(groups // 2)]
    return lax.all_gather(x, "tp", axis=0, tiled=False, axis_index_groups=chips)


def chip_exchange(pieces):
    groups = lax.axis_size("tp")
    chip = lax.axis_index("tp") // 2
    chips = pieces.shape[0]
    got = [lax.dynamic_index_in_dim(pieces, chip, 0, keepdims=False)]
    for k in range(1, chips):
        piece = lax.dynamic_index_in_dim(pieces, chip ^ k, 0, keepdims=False)
        got.append(lax.ppermute(piece, "tp", [(i, i ^ (2 * k)) for i in range(groups)]))
    return got


def gather_queries(queries):
    groups = lax.axis_size("tp")
    rows = queries.shape[0]
    split = queries.reshape(rows, groups // 2, -1)
    got = lax.all_to_all(
        split,
        "tp",
        split_axis=1,
        concat_axis=0,
        tiled=True,
        axis_index_groups=[[i for i in range(groups) if i % 2 == core] for core in (0, 1)],
    )
    return got.reshape(groups // 2 * rows, -1)


def share_queries(part, rows_local, me):
    rows, width = part.shape
    both = pair_gather(part).reshape(2, rows // rows_local, rows_local, 2, width // 2)
    mine = lax.dynamic_index_in_dim(both, me % 2, 3, keepdims=False)
    return mine.transpose(1, 0, 2, 3).reshape(2 * rows, width // 2)


def return_heads(mixed, me):
    groups = lax.axis_size("tp")
    rows, width = mixed.shape
    rows_local = rows // groups
    both = pair_gather(mixed)
    both = both.reshape(2, groups // 2, 2, rows_local, width)
    mine = lax.dynamic_index_in_dim(both, me % 2, 2, keepdims=False)
    return chip_exchange(mine.transpose(1, 0, 2, 3))


def add_new_kernel(dim, scale, chip_ref, query_ref, fresh_ref, *refs):
    pieces, out_ref = refs[:-1], refs[-1]
    heads, _, width = pieces[0].shape
    lanes = 128
    group = (width - lanes) // dim
    chip = chip_ref[0]
    lane = lax.broadcasted_iota(jnp.int32, (pieces[0].shape[1], lanes), 1)
    results = []
    for k, piece in enumerate(pieces):
        for h in range(heads):
            place = (chip ^ k) * heads + h
            fresh = pl.multiple_of(place * (2 * dim), 2 * dim)
            fresh_key = fresh_ref[:, pl.ds(fresh, dim)].astype(jnp.float32)
            fresh_value = fresh_ref[:, pl.ds(fresh + dim, dim)].astype(jnp.float32)
            parts = piece[h, :, group * dim :].astype(jnp.float32)
            level = parts
            for part in range(1, LEVEL_PARTS):
                level = level + pltpu.roll(parts, lanes - part * group, 1)
            own = jnp.zeros_like(level)
            places = []
            for j in range(group):
                places.append(pl.multiple_of(place * (group * dim) + j * dim, dim))
                query = query_ref[:, pl.ds(places[-1], dim)].astype(jnp.float32)
                score = jnp.sum(query * fresh_key, axis=1, keepdims=True) * scale
                own = jnp.where(lane == j, score, own)
            top = jnp.maximum(level, own)
            cached, new = jnp.exp(level - top), jnp.exp(own - top)
            total = cached + new
            cached, new = cached / total, new / total
            for j in range(group):
                value = piece[h, :, j * dim : (j + 1) * dim].astype(jnp.float32)
                mixed = value * cached[:, j : j + 1] + fresh_value * new[:, j : j + 1]
                results.append((places[j], mixed.astype(out_ref.dtype)))
    for at, mixed in results:
        out_ref[:, pl.ds(at, dim)] = mixed


def add_new_token(pieces, queries, new_kv, dim, scale):
    chip = (lax.axis_index("tp") // 2).astype(jnp.int32).reshape(1)
    vmem = pl.BlockSpec(memory_space=pltpu.VMEM)
    return pl.pallas_call(
        functools.partial(add_new_kernel, dim, scale),
        out_shape=jax.ShapeDtypeStruct(queries.shape, queries.dtype),
        in_specs=[pl.BlockSpec(memory_space=pltpu.SMEM)] + [vmem] * (2 + len(pieces)),
        out_specs=vmem,
        compiler_params=pltpu.CompilerParams(vmem_limit_bytes=16 * 1024 * 1024),
        cost_estimate=pl.CostEstimate(
            flops=8 * queries.size,
            bytes_accessed=4 * queries.size,
            transcendentals=2 * queries.size // dim,
        ),
        name="add_new_token",
    )(chip, queries, new_kv, *pieces)


def on_device(
    queries,
    new_kv,
    kv_pool,
    context_lens,
    block_table,
    send_pages,
    send_dest,
    recv_pool,
    recv_table,
):
    peers = lax.axis_size("inst")
    me = lax.axis_index("tp")
    _, pages, page_size, kv_local, width = kv_pool.shape
    dim = width // 2
    slots = recv_table.shape[1]
    pool = kv_pool.reshape(pages, page_size, width)

    query = gather_queries(queries)
    outgoing = pack_pages(pool, send_pages, send_dest.reshape(1, -1), peers, slots // peers)
    query, outgoing = lax.optimization_barrier((query, outgoing))
    order = sorted(range(peers), key=place_of)
    arrived = lax.all_to_all(
        outgoing, "inst", split_axis=0, concat_axis=0, tiled=True, axis_index_groups=[order]
    )

    owner = token_owners(context_lens, block_table, pages, page_size)
    scale = dim ** (-0.5)
    query = share_queries(query, queries.shape[0], me)
    mixed = attend(query, owner, pool.reshape(pages * page_size, width), scale)
    returned = return_heads(mixed, me)
    attended = add_new_token(returned, queries, new_kv, dim, scale)

    slot = jnp.arange(slots, dtype=jnp.int32)
    per_peer = slots // peers
    where_from = place_of(slot // per_peer) * per_peer + slot % per_peer
    source = jnp.sum(
        jnp.where(recv_table[0][None, :] == slot[:, None], where_from[None, :], 0), axis=1
    )
    mixed, recv_pool = lax.optimization_barrier((mixed, recv_pool))
    old = stage(recv_pool.reshape(slots, page_size, width))
    landed = land_pages(arrived, old, source)
    return (attended, landed.reshape(recv_pool.shape))


def solution(mesh):
    return jax.shard_map(
        on_device,
        mesh=mesh,
        in_specs=(
            P(("inst", "tp"), None),
            P(("inst", "tp"), None),
            P("inst", None, None, "tp", None),
            P("inst"),
            P("inst", None),
            P("inst", None),
            P("inst", None),
            P("inst", None, None, "tp", None),
            P("inst", None),
        ),
        out_specs=(P(("inst", "tp"), None), P("inst", None, None, "tp", None)),
        check_vma=False,
    )
```
